1024 devices in a mesh: rep: 64 (over z_hi, y, core), blk: 4 (over x), tp: 4 (over z_lo).
Axes of the slice: x: 4, y: 8, z: 16 (z_hi: 4, z_lo: 4; z = z_hi * 4 + z_lo), core: 2. Of those that a mesh axis runs over, the one named last changes fastest.
Arguments:
- hidden: bfloat16 [8192, 12288], P(('rep', 'blk', 'tp')), may hold values from -700 to 700
- projection_weight: bfloat16 [12288, 2048], P(('blk', 'tp')), may hold values from -1 to 1
- norm_gain: float32 [2048], replicated, may hold values from 0.5 to 1.5
- upstream: bfloat16 [8192, 2048], P('rep'), may hold values from -700 to 700
- loss_mask: int32 [8192], P('rep'), may hold values 0 or 1
Outputs:
- weight_grad: float32 [16, 768, 2048], P(('blk', 'tp'), 'rep')
- grad_norm: float32 [], replicated
The draws below stay inside these ranges and needn't reach their ends.
All inputs are finite; a program needn't handle non-finite values. No bound on the sum of `loss_mask` on one device may be relied on, other than what follows from the above.
Results may differ from the reference program's by a relative error of at most 0.0085.
Values may be sent and summed in bfloat16 or wider, within the bound.
No kernel may reach another device: no remote copies, remote signals or barrier semaphores. Data moves between devices by JAX's collectives and lax.ppermute only.
A program may use at most 64 MiB of HBM per device.

```python
import math
import jax
import jax.numpy as jnp
from jax import lax

D = 2048
JOINED = 12288
TOKENS = 8192
SHARD = 768


def spread(subkey, entries):
    return jnp.exp(jax.random.uniform(subkey, (entries,), jnp.float32, 0.0, math.log(10.0)))


def draw_hidden(key, part):
    key = jax.random.fold_in(key, 11)
    subkeys = jax.random.split(key, 3)
    normal_part = jnp.clip(jax.random.normal(subkeys[0], (TOKENS, JOINED), jnp.float32), -4.0, 4.0)
    rising = 3.0 ** (jnp.arange(JOINED, dtype=jnp.float32) / JOINED)
    column_scale = spread(subkeys[1], JOINED) * rising
    row_scale = spread(subkeys[2], TOKENS)[:, None]
    return (0.1 * normal_part * row_scale * column_scale).astype(jnp.bfloat16)


def draw_projection_weight(key, part):
    key = jax.random.fold_in(key, 23)
    subkeys = jax.random.split(key, 2)
    normal_part = jnp.clip(jax.random.normal(subkeys[0], (JOINED, D), jnp.float32), -4.0, 4.0)
    column_scale = spread(subkeys[1], D)
    return (normal_part * column_scale / math.sqrt(JOINED)).astype(jnp.bfloat16)


def draw_upstream(key, part):
    key = jax.random.fold_in(key, 37)
    subkeys = jax.random.split(key, 3)
    normal_part = jnp.clip(jax.random.normal(subkeys[0], (TOKENS, D), jnp.float32), -4.0, 4.0)
    rising = 3.0 ** (jnp.arange(TOKENS, dtype=jnp.float32) / TOKENS)
    row_scale = (spread(subkeys[1], TOKENS) * rising)[:, None]
    column_scale = spread(subkeys[2], D)
    return (0.1 * normal_part * row_scale * column_scale).astype(jnp.bfloat16)


def place_ends(array, rng, smallest, top_value):
    longest = array.shape.index(max(array.shape))
    spots = []
    for shift in (0, 1):
        where = [jax.random.randint(jax.random.fold_in(rng, axis), (), 0, length) for axis, length in enumerate(array.shape)]
        where[longest] = (where[longest] + shift) % array.shape[longest]
        spots.append(tuple(where))
    return array.at[spots[0]].set(smallest).at[spots[1]].set(top_value)


def setup_inputs(seed: int = 0) -> dict:
    key_of = jax.random.split(jax.random.key(seed), 6)
    hidden = draw_hidden(jax.random.fold_in(key_of[5], 71), 0)
    projection_weight = draw_projection_weight(jax.random.fold_in(key_of[5], 71), 0)
    norm_gain = jnp.clip(jax.random.uniform(key_of[2], (D,), jnp.float32, 0.5, 1.5), 0.5, 1.5)
    upstream = draw_upstream(jax.random.fold_in(key_of[5], 71), 0)
    loss_mask = place_ends((jax.random.randint(key_of[4], (TOKENS,), 0, 4) < 3).astype(jnp.int32), jax.random.fold_in(key_of[4], 1), 0, 1)
    return dict(hidden=hidden, projection_weight=projection_weight, norm_gain=norm_gain, upstream=upstream, loss_mask=loss_mask)


def norm_backward(projected, norm_gain, cotangent, token_mask):
    inverse_rms = lax.rsqrt(lax.optimization_barrier(jnp.mean(projected * projected, axis=1, keepdims=True)) + 1e-06)
    normed = projected * inverse_rms
    scaled = norm_gain * (cotangent.astype(jnp.float32) * token_mask.astype(jnp.float32)[:, None])
    along = lax.optimization_barrier(jnp.mean(scaled * normed, axis=1, keepdims=True))
    return (inverse_rms * (scaled - normed * along)).astype(jnp.bfloat16)

def reference(hidden, projection_weight, norm_gain, upstream, loss_mask):
    group_count = JOINED // SHARD

    def add_group(index, total):
        start = (index * SHARD).astype(jnp.int32)
        rows_in = lax.dynamic_slice_in_dim(hidden, start, SHARD, 1)
        weight_rows = lax.dynamic_slice_in_dim(projection_weight, start, SHARD, 0)
        partial_value = jnp.dot(rows_in, weight_rows, preferred_element_type=jnp.float32).astype(jnp.bfloat16)
        return total + partial_value.astype(jnp.float32)
    projected = lax.fori_loop(jnp.int32(0), jnp.int32(group_count), add_group, jnp.zeros((TOKENS, D), jnp.float32))
    token_grad = norm_backward(projected, norm_gain, upstream, loss_mask)
    grad_full = lax.dot_general(hidden, token_grad, (((0,), (0,)), ((), ())), preferred_element_type=jnp.float32)
    grad_norm = jnp.sqrt(jnp.sum(grad_full * grad_full))
    limit = jnp.sqrt(jnp.float32(JOINED * D))
    factor = jnp.minimum(1.0, limit / (grad_norm + 1e-06))
    return ((grad_full * factor).reshape(JOINED // SHARD, SHARD, D), grad_norm)
```

```python
import jax
import jax.numpy as jnp
import numpy as np
from jax import lax
from jax.sharding import Mesh, PartitionSpec as P

ZHI, YS, CORES = 4, 8, 2
REP = ("zh", "y", "core")
GROUP = ("blk", "tp")
BF16, F32 = jnp.bfloat16, jnp.float32


def norm_backward(projected, norm_gain, cotangent, token_mask):
    inverse_rms = lax.rsqrt(jnp.mean(projected * projected, axis=1, keepdims=True) + 1e-06)
    normed = projected * inverse_rms
    scaled = norm_gain * (cotangent.astype(F32) * token_mask.astype(F32)[:, None])
    along = jnp.mean(scaled * normed, axis=1, keepdims=True)
    return (inverse_rms * (scaled - normed * along)).astype(BF16)


def exchange(blocks, axes):
    return lax.all_to_all(blocks, axes, split_axis=0, concat_axis=0, tiled=True)


def total_over(value, axes, size):
    arrived = exchange(lax.optimization_barrier(jnp.full((size, 1, 128), value, F32)), axes)
    return jnp.sum(arrived[:, 0, 0])


def body(hidden, projection_weight, norm_gain, upstream, loss_mask):
    tok, joined = hidden.shape
    groups = lax.axis_size(GROUP)
    shard, width = projection_weight.shape
    own_rows = shard // (ZHI * YS * CORES)
    core = lax.axis_index("core")
    zh = lax.axis_index("zh")
    swap = [(0, 1), (1, 0)]

    sent = lax.optimization_barrier(hidden.reshape(tok, groups, shard).transpose(1, 0, 2))
    columns = exchange(sent, GROUP).reshape(groups * tok, shard)

    order = np.arange(shard).reshape(ZHI, YS, CORES, own_rows).transpose(2, 1, 0, 3).reshape(CORES, -1)
    kept = shard // CORES
    mine = jnp.asarray(order.astype(np.int32))
    feature = lax.broadcasted_iota(jnp.int32, (shard, kept), 0)
    pick_own = (feature == lax.dynamic_index_in_dim(mine, core, 0)).astype(BF16)
    pick_other = (feature == lax.dynamic_index_in_dim(mine, 1 - core, 0)).astype(BF16)
    own_cols = jnp.dot(columns, pick_own, preferred_element_type=F32).astype(BF16)
    give_cols = jnp.dot(columns, pick_other, preferred_element_type=F32).astype(BF16)
    got_cols = lax.ppermute(give_cols, "core", swap)

    partial_value = jnp.dot(columns, projection_weight, preferred_element_type=F32).astype(BF16)
    parts = exchange(lax.optimization_barrier(partial_value.reshape(groups, tok, width)), GROUP)
    projected = jnp.sum(parts.astype(F32), axis=0)
    offset = lax.axis_index(GROUP) * tok
    own_cotangent = lax.dynamic_slice_in_dim(upstream, offset, tok, 0)
    own_mask = lax.dynamic_slice_in_dim(loss_mask, offset, tok, 0)
    own_grad = norm_backward(projected, norm_gain, own_cotangent, own_mask)
    spread = lax.optimization_barrier(jnp.broadcast_to(own_grad[None], (groups, tok, width)))
    token_grad = exchange(spread, GROUP).reshape(groups * tok, width)
    other_grad = lax.ppermute(token_grad, "core", swap)

    contract = (((0,), (0,)), ((), ()))
    block = lax.dot_general(
        jnp.concatenate([own_cols, got_cols], 0),
        jnp.concatenate([token_grad, other_grad], 0),
        contract,
        preferred_element_type=F32,
    ).astype(BF16)
    by_y = exchange(lax.optimization_barrier(block.reshape(YS, ZHI * own_rows, width)), "y")
    over_y = jnp.sum(by_y.astype(F32), axis=0).reshape(ZHI, own_rows, width)

    total = lax.dynamic_index_in_dim(over_y, zh, 0, keepdims=False)
    for step in (2, 1, 3):
        piece = lax.dynamic_index_in_dim(over_y, (zh + step) % ZHI, 0, keepdims=False).astype(BF16)
        total = total + lax.ppermute(
            piece, "zh", [(i, (i + step) % ZHI) for i in range(ZHI)]
        ).astype(F32)

    squares = total_over(jnp.sum(total * total), ("core", "blk", "tp"), CORES * groups)
    squares = total_over(squares, ("zh", "y"), ZHI * YS)
    grad_norm = jnp.sqrt(squares)
    limit = jnp.sqrt(jnp.float32(joined * width))
    factor = jnp.minimum(1.0, limit / (grad_norm + 1e-06))
    return ((total * factor)[None], grad_norm)


def solution(mesh):
    sizes = (ZHI, YS, CORES, mesh.shape["blk"], mesh.shape["tp"])
    fine = Mesh(mesh.devices.reshape(sizes), REP + GROUP)
    return jax.shard_map(
        body,
        mesh=fine,
        in_specs=(
            P(REP + GROUP, None),
            P(GROUP, None),
            P(),
            P(REP, None),
            P(REP),
        ),
        out_specs=(P(GROUP, REP, None), P()),
        check_vma=False,
    )
```

```python
import jax
import jax.numpy as jnp
from jax import lax
from jax.sharding import Mesh, PartitionSpec as P

ZHI, YS, CORES = 4, 8, 2
REP = ("zh", "y", "core")
GROUP = ("blk", "tp")
BF16, F32 = jnp.bfloat16, jnp.float32


def norm_backward(projected, norm_gain, cotangent, token_mask):
    inverse_rms = lax.rsqrt(jnp.mean(projected * projected, axis=1, keepdims=True) + 1e-06)
    normed = projected * inverse_rms
    scaled = norm_gain * (cotangent.astype(F32) * token_mask.astype(F32)[:, None])
    along = jnp.mean(scaled * normed, axis=1, keepdims=True)
    return (inverse_rms * (scaled - normed * along)).astype(BF16)


def exchange(blocks, axes):
    return lax.all_to_all(blocks, axes, split_axis=0, concat_axis=0, tiled=True)


def total_over(value, axes, size):
    arrived = exchange(lax.optimization_barrier(jnp.full((size, 1, 128), value, F32)), axes)
    return jnp.sum(arrived[:, 0, 0])


def body(hidden, projection_weight, norm_gain, upstream, loss_mask):
    tok, joined = hidden.shape
    groups = lax.axis_size(GROUP)
    shard, width = projection_weight.shape
    slices = YS * CORES
    part = width // slices

    sent = lax.optimization_barrier(hidden.reshape(tok, groups, shard).transpose(1, 0, 2))
    columns = exchange(sent, GROUP).reshape(groups * tok, shard)
    all_columns = lax.all_gather(columns, ("y", "core"), axis=0, tiled=True)

    partial_value = jnp.dot(columns, projection_weight, preferred_element_type=F32).astype(BF16)
    parts = exchange(lax.optimization_barrier(partial_value.reshape(groups, tok, width)), GROUP)
    projected = jnp.sum(parts.astype(F32), axis=0)
    offset = lax.axis_index(GROUP) * tok
    own_cotangent = lax.dynamic_slice_in_dim(upstream, offset, tok, 0)
    own_mask = lax.dynamic_slice_in_dim(loss_mask, offset, tok, 0)
    own_grad = norm_backward(projected, norm_gain, own_cotangent, own_mask)

    cut = lax.optimization_barrier(own_grad.reshape(tok, slices, part).transpose(1, 0, 2))
    cut = exchange(cut, ("y", "core"))
    spread = lax.optimization_barrier(jnp.broadcast_to(cut[None], (groups, slices, tok, part)))
    arrived = exchange(spread, GROUP)
    token_grad = arrived.transpose(1, 0, 2, 3).reshape(slices * groups * tok, part)

    contract = (((0,), (0,)), ((), ()))
    block = lax.dot_general(all_columns, token_grad, contract, preferred_element_type=F32).astype(BF16)
    by_zh = exchange(lax.optimization_barrier(block.reshape(ZHI, shard // ZHI, part)), "zh")
    over_zh = jnp.sum(by_zh.astype(F32), axis=0)

    own_rows = shard // (ZHI * slices)
    squares = jnp.full((slices, 1, part), jnp.sum(over_zh * over_zh), F32)
    spare = jnp.zeros((slices, 16 - own_rows - 1, part), F32)
    rows = jnp.concatenate([over_zh.reshape(slices, own_rows, part), squares, spare], axis=1)
    back = exchange(lax.optimization_barrier(rows), ("y", "core"))
    total = back[:, :own_rows].transpose(1, 0, 2).reshape(own_rows, width)
    squares = jnp.sum(back[:, own_rows, 0])
    squares = total_over(squares, ("zh", "blk", "tp"), ZHI * groups)
    grad_norm = jnp.sqrt(squares)
    limit = jnp.sqrt(jnp.float32(joined * width))
    factor = jnp.minimum(1.0, limit / (grad_norm + 1e-06))
    return ((total * factor)[None], grad_norm)


def solution(mesh):
    sizes = (ZHI, YS, CORES, mesh.shape["blk"], mesh.shape["tp"])
    fine = Mesh(mesh.devices.reshape(sizes), REP + GROUP)
    return jax.shard_map(
        body,
        mesh=fine,
        in_specs=(
            P(REP + GROUP, None),
            P(GROUP, None),
            P(),
            P(REP, None),
            P(REP),
        ),
        out_specs=(P(GROUP, REP, None), P()),
        check_vma=False,
    )
```

```python
import functools

import jax
import jax.numpy as jnp
from jax import lax
from jax.experimental import pallas as pl
from jax.experimental.pallas import tpu as pltpu
from jax.sharding import Mesh, PartitionSpec as P

ZHI, YS, CORES = 4, 8, 2
REP = ("zh", "y", "core")
ALONG = ("y", "core")
GROUP = ("blk", "tp")
LANES = 128
BF16, F32 = jnp.bfloat16, jnp.float32


def exchange(blocks, axes):
    return lax.all_to_all(blocks, axes, split_axis=0, concat_axis=0, tiled=True)


def norm_backward_kernel(parts_ref, scaled_ref, out_ref):
    groups = parts_ref.shape[0]
    projected = parts_ref[0].astype(F32)
    for g in range(1, groups):
        projected += parts_ref[g].astype(F32)
    scaled = scaled_ref[...]
    inverse_rms = lax.rsqrt(jnp.mean(projected * projected, axis=1, keepdims=True) + 1e-06)
    normed = projected * inverse_rms
    along = jnp.mean(scaled * normed, axis=1, keepdims=True)
    token_grad = (inverse_rms * (scaled - normed * along)).astype(BF16)
    for j in range(out_ref.shape[0]):
        out_ref[j] = token_grad[:, j * LANES : (j + 1) * LANES]


def norm_backward(parts, scaled, slices):
    _, tok, width = parts.shape
    return pl.pallas_call(
        norm_backward_kernel,
        out_shape=jax.ShapeDtypeStruct((slices, tok, width // slices), BF16),
        name="norm_backward",
    )(parts, scaled)


def product_kernel(columns_ref, grads_ref, out_ref, total_ref):
    step = pl.program_id(0)

    @pl.when(step == 0)
    def _():
        total_ref[...] = jnp.zeros_like(total_ref)

    groups, chunk, tok, part = grads_ref.shape
    grads = grads_ref[...].astype(F32).transpose(1, 0, 2, 3).reshape(chunk * groups * tok, part)
    total_ref[...] += jnp.dot(grads.T.astype(BF16), columns_ref[...], preferred_element_type=F32)

    @pl.when(step == pl.num_programs(0) - 1)
    def _():
        out_ref[...] = total_ref[...].T.astype(BF16)


def product(all_columns, arrived, steps):
    groups, slices, tok, part = arrived.shape
    tokens, shard = all_columns.shape
    return pl.pallas_call(
        product_kernel,
        grid=(steps,),
        in_specs=[
            pl.BlockSpec((tokens // steps, shard), lambda i: (i, 0)),
            pl.BlockSpec((groups, slices // steps, tok, part), lambda i: (0, i, 0, 0)),
        ],
        out_specs=pl.BlockSpec((shard, part), lambda i: (0, 0)),
        out_shape=jax.ShapeDtypeStruct((shard, part), BF16),
        scratch_shapes=[pltpu.VMEM((part, shard), F32)],
        name="product",
    )(all_columns, arrived)


def gather_rows_kernel(own_rows, pieces_ref, out_ref):
    total = pieces_ref[0].astype(F32)
    for k in range(1, pieces_ref.shape[0]):
        total += pieces_ref[k].astype(F32)
    slices, padded, part = out_ref.shape
    squares = jnp.full((padded - own_rows, part), jnp.sum(total * total), F32)
    for j in range(slices):
        out_ref[j, :own_rows] = total[j * own_rows : (j + 1) * own_rows]
        out_ref[j, own_rows:] = squares


def gather_rows(pieces, own_rows, slices, padded):
    return pl.pallas_call(
        functools.partial(gather_rows_kernel, own_rows),
        out_shape=jax.ShapeDtypeStruct((slices, padded, pieces.shape[2]), F32),
        name="gather_rows",
    )(pieces)


def squares_kernel(own_rows, back_ref, out_ref):
    total = jnp.sum(back_ref[:, own_rows : own_rows + 1, :], axis=0)
    out_ref[...] = jnp.broadcast_to(total[None], out_ref.shape)


def spread_squares(back, own_rows, size):
    return pl.pallas_call(
        functools.partial(squares_kernel, own_rows),
        out_shape=jax.ShapeDtypeStruct((size, 1, back.shape[2]), F32),
        name="spread_squares",
    )(back)


def clip_kernel(limit_square, back_ref, squares_ref, out_ref, norm_ref):
    squares = jnp.sum(squares_ref[...], axis=0)
    norm = jnp.sqrt(squares)
    factor = jnp.minimum(1.0, jnp.sqrt(jnp.full_like(norm, limit_square)) / (norm + 1e-06))
    norm_ref[0, 0] = jnp.max(norm)
    slices, _, part = back_ref.shape
    for j in range(slices):
        for r in range(out_ref.shape[0]):
            out_ref[r, :, j * part : (j + 1) * part] = back_ref[j, r : r + 1, :] * factor


def clip(back, squares, own_rows, width, limit_square):
    return pl.pallas_call(
        functools.partial(clip_kernel, limit_square),
        out_shape=(
            jax.ShapeDtypeStruct((own_rows, 1, width), F32),
            jax.ShapeDtypeStruct((1, 1), F32),
        ),
        out_specs=(
            pl.BlockSpec(memory_space=pltpu.VMEM),
            pl.BlockSpec(memory_space=pltpu.SMEM),
        ),
        name="clip",
    )(back, squares)


def body(hidden, projection_weight, norm_gain, upstream, loss_mask):
    tok, joined = hidden.shape
    groups = lax.axis_size(GROUP)
    shard, width = projection_weight.shape
    slices = YS * CORES
    part = width // slices
    own_rows = shard // (ZHI * slices)

    sent = lax.optimization_barrier(hidden.reshape(tok, groups, shard).transpose(1, 0, 2))
    columns = exchange(sent, GROUP).reshape(groups * tok, shard)
    all_columns = lax.all_gather(columns, ALONG, axis=0, tiled=True)

    partial_value = jnp.dot(columns, projection_weight, preferred_element_type=F32).astype(BF16)
    parts = exchange(lax.optimization_barrier(partial_value.reshape(groups, tok, width)), GROUP)
    offset = lax.axis_index(GROUP) * tok
    own_cotangent = lax.dynamic_slice_in_dim(upstream, offset, tok, 0)
    own_mask = lax.dynamic_slice_in_dim(loss_mask, offset, tok, 0)
    scaled = norm_gain * (own_cotangent.astype(F32) * own_mask.astype(F32)[:, None])

    cut = exchange(norm_backward(parts, scaled, slices), ALONG)
    spread = lax.optimization_barrier(jnp.broadcast_to(cut[None], (groups, slices, tok, part)))
    arrived = exchange(spread, GROUP)
    block = product(all_columns, arrived, 4)
    by_zh = exchange(block.reshape(ZHI, shard // ZHI, part), "zh")

    back = exchange(gather_rows(by_zh, own_rows, slices, 16), ALONG)
    squares = exchange(spread_squares(back, own_rows, ZHI * groups), ("zh",) + GROUP)
    rows, grad_norm = clip(back, squares, own_rows, width, float(joined * width))
    return (rows.transpose(1, 0, 2), grad_norm.reshape(()))


def solution(mesh):
    sizes = (ZHI, YS, CORES, mesh.shape["blk"], mesh.shape["tp"])
    fine = Mesh(mesh.devices.reshape(sizes), REP + GROUP)
    return jax.shard_map(
        body,
        mesh=fine,
        in_specs=(
            P(REP + GROUP, None),
            P(GROUP, None),
            P(),
            P(REP, None),
            P(REP),
        ),
        out_specs=(P(GROUP, REP, None), P()),
        check_vma=False,
    )
```

```python
import functools

import jax
import jax.numpy as jnp
from jax import lax
from jax.experimental import pallas as pl
from jax.experimental.pallas import tpu as pltpu
from jax.sharding import Mesh, PartitionSpec as P

ZHI, YS, CORES = 4, 8, 2
REP = ("zh", "y", "core")
ALONG = ("y", "core")
GROUP = ("blk", "tp")
EARLY = (3, 5, 2, 6)
BF16, F32 = jnp.bfloat16, jnp.float32


def exchange(blocks, axes):
    return lax.all_to_all(blocks, axes, split_axis=0, concat_axis=0, tiled=True)


def norm_backward_kernel(parts_ref, scaled_ref, out_ref):
    groups = parts_ref.shape[0]
    projected = parts_ref[0].astype(F32)
    for g in range(1, groups):
        projected += parts_ref[g].astype(F32)
    scaled = scaled_ref[...]
    inverse_rms = lax.rsqrt(jnp.mean(projected * projected, axis=1, keepdims=True) + 1e-06)
    normed = projected * inverse_rms
    along = jnp.mean(scaled * normed, axis=1, keepdims=True)
    token_grad = (inverse_rms * (scaled - normed * along)).astype(BF16)
    part = out_ref.shape[2]
    for j in range(out_ref.shape[0]):
        out_ref[j] = token_grad[:, j * part : (j + 1) * part]


def norm_backward(parts, scaled, slices):
    _, tok, width = parts.shape
    return pl.pallas_call(
        norm_backward_kernel,
        out_shape=jax.ShapeDtypeStruct((slices, tok, width // slices), BF16),
        name="norm_backward",
    )(parts, scaled)


def product_kernel(place_ref, *refs):
    column_refs, (grads_ref, keep_ref, give_ref, total_ref) = refs[:YS], refs[YS:]
    y, core = place_ref[0], place_ref[1]
    groups, _, tok, cols = grads_ref.shape
    part = keep_ref.shape[1]
    for step in range(YS):
        source = lax.rem(y + (YS - step), YS)
        grads = grads_ref[:, source].astype(F32).reshape(groups * tok, cols)
        term = jnp.dot(grads.T.astype(BF16), column_refs[step][...], preferred_element_type=F32)
        if step == 0:
            total_ref[...] = term
        else:
            total_ref[...] += term
    keep_ref[...] = total_ref[pl.ds(pl.multiple_of(core * part, part), part)].T
    give_ref[...] = total_ref[pl.ds(pl.multiple_of((1 - core) * part, part), part)].T.astype(BF16)


def product(chunks, arrived, place):
    groups, _, tok, cols = arrived.shape
    shard = chunks[0].shape[1]
    half = (shard, cols // CORES)
    return pl.pallas_call(
        product_kernel,
        in_specs=[pl.BlockSpec(memory_space=pltpu.SMEM)]
        + [pl.BlockSpec(memory_space=pltpu.VMEM)] * (YS + 1),
        out_shape=(jax.ShapeDtypeStruct(half, F32), jax.ShapeDtypeStruct(half, BF16)),
        scratch_shapes=[pltpu.VMEM((cols, shard), F32)],
        name="product",
    )(place, *chunks, arrived)


def gather_rows_kernel(own_rows, pieces_ref, out_ref):
    total = pieces_ref[0].astype(F32)
    for k in range(1, pieces_ref.shape[0]):
        total += pieces_ref[k].astype(F32)
    slices, padded, part = out_ref.shape
    squares = jnp.full((padded - own_rows, part), jnp.sum(total * total), F32)
    for j in range(slices):
        out_ref[j, :own_rows] = total[j * own_rows : (j + 1) * own_rows]
        out_ref[j, own_rows:] = squares


def gather_rows(pieces, own_rows, slices, padded):
    return pl.pallas_call(
        functools.partial(gather_rows_kernel, own_rows),
        out_shape=jax.ShapeDtypeStruct((slices, padded, pieces.shape[2]), F32),
        name="gather_rows",
    )(pieces)


def squares_kernel(own_rows, back_ref, out_ref):
    total = jnp.sum(back_ref[:, own_rows : own_rows + 1, :], axis=0)
    out_ref[...] = jnp.broadcast_to(total[None], out_ref.shape)


def spread_squares(back, own_rows, size):
    return pl.pallas_call(
        functools.partial(squares_kernel, own_rows),
        out_shape=jax.ShapeDtypeStruct((size, 1, back.shape[2]), F32),
        name="spread_squares",
    )(back)


def clip_kernel(limit_square, back_ref, squares_ref, out_ref, norm_ref):
    squares = jnp.sum(squares_ref[...], axis=0)
    norm = jnp.sqrt(squares)
    factor = jnp.minimum(1.0, jnp.sqrt(jnp.full_like(norm, limit_square)) / (norm + 1e-06))
    norm_ref[0, 0] = jnp.max(norm)
    slices, _, part = back_ref.shape
    for j in range(slices):
        for r in range(out_ref.shape[0]):
            out_ref[r, :, j * part : (j + 1) * part] = back_ref[j, r : r + 1, :] * factor


def clip(back, squares, own_rows, width, limit_square):
    return pl.pallas_call(
        functools.partial(clip_kernel, limit_square),
        out_shape=(
            jax.ShapeDtypeStruct((own_rows, 1, width), F32),
            jax.ShapeDtypeStruct((1, 1), F32),
        ),
        out_specs=(
            pl.BlockSpec(memory_space=pltpu.VMEM),
            pl.BlockSpec(memory_space=pltpu.SMEM),
        ),
        name="clip",
    )(back, squares)


def body(hidden, projection_weight, norm_gain, upstream, loss_mask):
    tok, joined = hidden.shape
    groups = lax.axis_size(GROUP)
    shard, width = projection_weight.shape
    slices = YS * CORES
    part = width // slices
    own_rows = shard // (ZHI * slices)

    sent = lax.optimization_barrier(hidden.reshape(tok, groups, shard).transpose(1, 0, 2))
    columns = exchange(sent, GROUP).reshape(groups * tok, shard)
    chunks = {0: columns}
    for step in EARLY + (4, 1, 7):
        chunks[step] = lax.ppermute(columns, "y", [(i, (i + step) % YS) for i in range(YS)])

    partial_value = jnp.dot(columns, projection_weight, preferred_element_type=F32).astype(BF16)
    parts = exchange(lax.optimization_barrier(partial_value.reshape(groups, tok, width)), GROUP)
    offset = lax.axis_index(GROUP) * tok
    own_cotangent = lax.dynamic_slice_in_dim(upstream, offset, tok, 0)
    own_mask = lax.dynamic_slice_in_dim(loss_mask, offset, tok, 0)
    scaled = norm_gain * (own_cotangent.astype(F32) * own_mask.astype(F32)[:, None])

    cut = exchange(norm_backward(parts, scaled, YS), "y")
    cut, *early = lax.optimization_barrier((cut, *(chunks[step] for step in EARLY)))
    for step, chunk in zip(EARLY, early):
        chunks[step] = chunk
    spread = lax.optimization_barrier(jnp.broadcast_to(cut[None], (groups, YS, tok, CORES * part)))
    arrived = exchange(spread, GROUP)
    place = jnp.stack([lax.axis_index("y"), lax.axis_index("core")]).astype(jnp.int32)
    keep, give = product([chunks[step] for step in range(YS)], arrived, place)
    block = (keep + lax.ppermute(give, "core", [(0, 1), (1, 0)]).astype(F32)).astype(BF16)
    by_zh = exchange(block.reshape(ZHI, shard // ZHI, part), "zh")

    back = exchange(gather_rows(by_zh, own_rows, slices, 16), ALONG)
    squares = exchange(spread_squares(back, own_rows, ZHI * groups), ("zh",) + GROUP)
    rows, grad_norm = clip(back, squares, own_rows, width, float(joined * width))
    return (rows.transpose(1, 0, 2), grad_norm.reshape(()))


def solution(mesh):
    sizes = (ZHI, YS, CORES, mesh.shape["blk"], mesh.shape["tp"])
    fine = Mesh(mesh.devices.reshape(sizes), REP + GROUP)
    return jax.shard_map(
        body,
        mesh=fine,
        in_specs=(
            P(REP + GROUP, None),
            P(GROUP, None),
            P(),
            P(REP, None),
            P(REP),
        ),
        out_specs=(P(GROUP, REP, None), P()),
        check_vma=False,
    )
```

```python
import functools

import jax
import jax.numpy as jnp
from jax import lax
from jax.experimental import pallas as pl
from jax.experimental.pallas import tpu as pltpu
from jax.sharding import Mesh, PartitionSpec as P

ZHI, QS, PS, CORES = 4, 4, 2, 2
REP = ("zh", "q", "p", "core")
NEAR = ("q", "core")
ALONG = ("q", "p", "core")
GROUP = ("blk", "tp")
PAIR = [(0, 1), (1, 0)]
BF16, F32 = jnp.bfloat16, jnp.float32


def exchange(blocks, axes):
    return lax.all_to_all(blocks, axes, split_axis=0, concat_axis=0, tiled=True)


def norm_backward_kernel(parts_ref, scaled_ref, out_ref):
    groups = parts_ref.shape[0]
    projected = parts_ref[0].astype(F32)
    for g in range(1, groups):
        projected += parts_ref[g].astype(F32)
    scaled = scaled_ref[...]
    inverse_rms = lax.rsqrt(jnp.mean(projected * projected, axis=1, keepdims=True) + 1e-06)
    normed = projected * inverse_rms
    along = jnp.mean(scaled * normed, axis=1, keepdims=True)
    token_grad = (inverse_rms * (scaled - normed * along)).astype(BF16)
    part = out_ref.shape[2]
    for j in range(out_ref.shape[0]):
        out_ref[j] = token_grad[:, j * part : (j + 1) * part]


def norm_backward(parts, scaled, slices):
    _, tok, width = parts.shape
    return pl.pallas_call(
        norm_backward_kernel,
        out_shape=jax.ShapeDtypeStruct((slices, tok, width // slices), BF16),
        name="norm_backward",
    )(parts, scaled)


def product_kernel(place_ref, own_ref, other_ref, grads_ref, keep_ref, give_ref, rows_ref, total_ref):
    q, p, core = place_ref[0], place_ref[1], place_ref[2]
    groups, _, _, tok, part = grads_ref.shape
    for step in range(QS):
        source = lax.rem(q + (QS - step), QS)
        for place, columns_ref in ((core, own_ref), (1 - core, other_ref)):
            grads = grads_ref[:, source, place].astype(F32).reshape(groups * tok, part)
            term = jnp.dot(grads.T.astype(BF16), columns_ref[step], preferred_element_type=F32)
            if step == 0 and columns_ref is own_ref:
                total_ref[...] = term
            else:
                total_ref[...] += term
    rows_ref[...] = total_ref[...].T.reshape(rows_ref.shape)
    keep_ref[...] = rows_ref[:, p].reshape(keep_ref.shape)
    give_ref[...] = rows_ref[:, 1 - p].reshape(give_ref.shape).astype(BF16)


def product(own, other, arrived, place, own_rows):
    part = arrived.shape[-1]
    shard = own.shape[2]
    half = (shard // PS, part)
    return pl.pallas_call(
        product_kernel,
        in_specs=[pl.BlockSpec(memory_space=pltpu.SMEM)]
        + [pl.BlockSpec(memory_space=pltpu.VMEM)] * 3,
        out_shape=(jax.ShapeDtypeStruct(half, F32), jax.ShapeDtypeStruct(half, BF16)),
        scratch_shapes=[
            pltpu.VMEM((ZHI * QS, PS, CORES * own_rows, part), F32),
            pltpu.VMEM((part, shard), F32),
        ],
        name="product",
    )(place, own, other, arrived)


def gather_rows_kernel(own_rows, pieces_ref, out_ref):
    total = pieces_ref[0].astype(F32)
    for k in range(1, pieces_ref.shape[0]):
        total += pieces_ref[k].astype(F32)
    slices, padded, part = out_ref.shape
    squares = jnp.full((padded - own_rows, part), jnp.sum(total * total), F32)
    for j in range(slices):
        k = (j // (PS * CORES)) * CORES + j % CORES
        out_ref[j, :own_rows] = total[k * own_rows : (k + 1) * own_rows]
        out_ref[j, own_rows:] = squares


def gather_rows(pieces, own_rows, slices, padded):
    return pl.pallas_call(
        functools.partial(gather_rows_kernel, own_rows),
        out_shape=jax.ShapeDtypeStruct((slices, padded, pieces.shape[2]), F32),
        name="gather_rows",
    )(pieces)


def squares_kernel(own_rows, back_ref, out_ref):
    total = jnp.sum(back_ref[:, own_rows : own_rows + 1, :], axis=0)
    out_ref[...] = jnp.broadcast_to(total[None, :, : out_ref.shape[2]], out_ref.shape)


def spread_squares(back, own_rows, size):
    return pl.pallas_call(
        functools.partial(squares_kernel, own_rows),
        out_shape=jax.ShapeDtypeStruct((size, 1, 128), F32),
        name="spread_squares",
    )(back)


def clip_kernel(limit_square, place_ref, back_ref, squares_ref, out_ref, norm_ref):
    squares = jnp.sum(squares_ref[...], axis=0)
    norm = jnp.sqrt(squares)
    factor = jnp.minimum(1.0, jnp.sqrt(jnp.full_like(norm, limit_square)) / (norm + 1e-06))
    norm_ref[0, 0] = jnp.max(norm)
    factor = jnp.concatenate([factor] * (back_ref.shape[2] // factor.shape[1]), axis=1)
    part = back_ref.shape[2]
    p = place_ref[1]
    for k in range(QS * CORES):
        rows = back_ref[(k // CORES) * (PS * CORES) + p * CORES + k % CORES]
        for r in range(out_ref.shape[0]):
            out_ref[r, :, k * part : (k + 1) * part] = rows[r : r + 1, :] * factor


def clip(place, back, squares, own_rows, width, limit_square):
    return pl.pallas_call(
        functools.partial(clip_kernel, limit_square),
        out_shape=(
            jax.ShapeDtypeStruct((own_rows, 1, width), F32),
            jax.ShapeDtypeStruct((1, 1), F32),
        ),
        in_specs=[
            pl.BlockSpec(memory_space=pltpu.SMEM),
            pl.BlockSpec(memory_space=pltpu.VMEM),
            pl.BlockSpec(memory_space=pltpu.VMEM),
        ],
        out_specs=(
            pl.BlockSpec(memory_space=pltpu.VMEM),
            pl.BlockSpec(memory_space=pltpu.SMEM),
        ),
        name="clip",
    )(place, back, squares)


def body(hidden, projection_weight, norm_gain, upstream, loss_mask):
    tok, joined = hidden.shape
    groups = lax.axis_size(GROUP)
    shard, width = projection_weight.shape
    slices = QS * CORES
    part = width // slices
    own_rows = shard // (ZHI * slices * PS)
    place = jnp.stack([lax.axis_index(axis) for axis in ALONG]).astype(jnp.int32)

    sent = lax.optimization_barrier(hidden.reshape(tok, groups, shard).transpose(1, 0, 2))
    columns = exchange(sent, GROUP).reshape(groups * tok, shard)
    chunks = {0: columns}
    for step in (2, 1, 3):
        chunks[step] = lax.ppermute(columns, "q", [(i, (i + step) % QS) for i in range(QS)])

    partial_value = jnp.dot(columns, projection_weight, preferred_element_type=F32).astype(BF16)
    parts = exchange(lax.optimization_barrier(partial_value.reshape(groups, tok, width)), GROUP)
    offset = lax.axis_index(GROUP) * tok
    own_cotangent = lax.dynamic_slice_in_dim(upstream, offset, tok, 0)
    own_mask = lax.dynamic_slice_in_dim(loss_mask, offset, tok, 0)
    scaled = norm_gain * (own_cotangent.astype(F32) * own_mask.astype(F32)[:, None])

    cut = exchange(norm_backward(parts, scaled, slices), NEAR)
    cut, *own_columns = lax.optimization_barrier((cut, *(chunks[step] for step in range(QS))))
    own_columns = jnp.stack(own_columns)
    other_columns = lax.ppermute(own_columns, "core", PAIR)
    spread = lax.optimization_barrier(jnp.broadcast_to(cut[None], (groups, slices, tok, part)))
    arrived = exchange(spread, GROUP).reshape(groups, QS, CORES, tok, part)
    keep, give = product(own_columns, other_columns, arrived, place, own_rows)
    block = (keep + lax.ppermute(give, "p", PAIR).astype(F32)).astype(BF16)
    by_zh = exchange(block.reshape(ZHI, slices * own_rows, part), "zh")

    back = exchange(gather_rows(by_zh, own_rows, slices * PS, 16), ALONG)
    squares = exchange(spread_squares(back, own_rows, ZHI * groups), ("zh",) + GROUP)
    rows, grad_norm = clip(place, back, squares, own_rows, width, float(joined * width))
    return (rows.transpose(1, 0, 2), grad_norm.reshape(()))


def solution(mesh):
    sizes = (ZHI, QS, PS, CORES, mesh.shape["blk"], mesh.shape["tp"])
    fine = Mesh(mesh.devices.reshape(sizes), REP + GROUP)
    return jax.shard_map(
        body,
        mesh=fine,
        in_specs=(
            P(REP + GROUP, None),
            P(GROUP, None),
            P(),
            P(REP, None),
            P(REP),
        ),
        out_specs=(P(GROUP, REP, None), P()),
        check_vma=False,
    )
```

```python
import functools

import jax
import jax.numpy as jnp
from jax import lax
from jax.experimental import pallas as pl
from jax.experimental.pallas import tpu as pltpu
from jax.sharding import Mesh, PartitionSpec as P

ZHI, YS, CORES = 4, 8, 2
REP = ("zh", "y", "core")
ALONG = ("y", "core")
GROUP = ("blk", "tp")
LANES = 128
BF16, F32 = jnp.bfloat16, jnp.float32


def exchange(blocks, axes):
    return lax.all_to_all(blocks, axes, split_axis=0, concat_axis=0, tiled=True)


def norm_backward_kernel(parts_ref, scaled_ref, out_ref):
    groups = parts_ref.shape[0]
    projected = parts_ref[0].astype(F32)
    for g in range(1, groups):
        projected += parts_ref[g].astype(F32)
    scaled = scaled_ref[...]
    inverse_rms = lax.rsqrt(jnp.mean(projected * projected, axis=1, keepdims=True) + 1e-06)
    normed = projected * inverse_rms
    along = jnp.mean(scaled * normed, axis=1, keepdims=True)
    token_grad = (inverse_rms * (scaled - normed * along)).astype(BF16)
    for j in range(out_ref.shape[0]):
        out_ref[j] = token_grad[:, j * LANES : (j + 1) * LANES]


def norm_backward(parts, scaled, slices):
    _, tok, width = parts.shape
    return pl.pallas_call(
        norm_backward_kernel,
        out_shape=jax.ShapeDtypeStruct((slices, tok, width // slices), BF16),
        compiler_params=pltpu.CompilerParams(vmem_limit_bytes=12 << 20),
        name="norm_backward",
    )(parts, scaled)


def product_kernel(columns_ref, grads_ref, out_ref, total_ref):
    step = pl.program_id(0)

    @pl.when(step == 0)
    def _():
        total_ref[...] = jnp.zeros_like(total_ref)

    groups, chunk, tok, part = grads_ref.shape
    grads = grads_ref[...].astype(F32).transpose(1, 0, 2, 3).reshape(chunk * groups * tok, part)
    total_ref[...] += jnp.dot(grads.T.astype(BF16), columns_ref[...], preferred_element_type=F32)

    @pl.when(step == pl.num_programs(0) - 1)
    def _():
        out_ref[...] = total_ref[...].T.astype(BF16)


def product(all_columns, arrived, steps):
    groups, slices, tok, part = arrived.shape
    tokens, shard = all_columns.shape
    return pl.pallas_call(
        product_kernel,
        grid=(steps,),
        in_specs=[
            pl.BlockSpec((tokens // steps, shard), lambda i: (i, 0)),
            pl.BlockSpec((groups, slices // steps, tok, part), lambda i: (0, i, 0, 0)),
        ],
        out_specs=pl.BlockSpec((shard, part), lambda i: (0, 0)),
        out_shape=jax.ShapeDtypeStruct((shard, part), BF16),
        scratch_shapes=[pltpu.VMEM((part, shard), F32)],
        name="product",
    )(all_columns, arrived)


def gather_rows_kernel(own_rows, pieces_ref, out_ref):
    total = pieces_ref[0].astype(F32)
    for k in range(1, pieces_ref.shape[0]):
        total += pieces_ref[k].astype(F32)
    slices, padded, part = out_ref.shape
    squares = jnp.full((padded - own_rows, part), jnp.sum(total * total), F32)
    for j in range(slices):
        out_ref[j, :own_rows] = total[j * own_rows : (j + 1) * own_rows]
        out_ref[j, own_rows:] = squares


def gather_rows(pieces, own_rows, slices, padded):
    return pl.pallas_call(
        functools.partial(gather_rows_kernel, own_rows),
        out_shape=jax.ShapeDtypeStruct((slices, padded, pieces.shape[2]), F32),
        compiler_params=pltpu.CompilerParams(vmem_limit_bytes=12 << 20),
        name="gather_rows",
    )(pieces)


def squares_kernel(own_rows, back_ref, out_ref):
    total = jnp.sum(back_ref[:, own_rows : own_rows + 1, :], axis=0)
    out_ref[...] = jnp.broadcast_to(total[None], out_ref.shape)


def spread_squares(back, own_rows, size):
    return pl.pallas_call(
        functools.partial(squares_kernel, own_rows),
        out_shape=jax.ShapeDtypeStruct((size, 1, back.shape[2]), F32),
        compiler_params=pltpu.CompilerParams(vmem_limit_bytes=12 << 20),
        name="spread_squares",
    )(back)


def clip_kernel(limit_square, back_ref, squares_ref, out_ref, norm_ref):
    squares = jnp.sum(squares_ref[...], axis=0)
    norm = jnp.sqrt(squares)
    factor = jnp.minimum(1.0, jnp.sqrt(jnp.full_like(norm, limit_square)) / (norm + 1e-06))
    norm_ref[0, 0] = jnp.max(norm)
    slices, _, part = back_ref.shape
    for j in range(slices):
        for r in range(out_ref.shape[0]):
            out_ref[r, :, j * part : (j + 1) * part] = back_ref[j, r : r + 1, :] * factor


def clip(back, squares, own_rows, width, limit_square):
    return pl.pallas_call(
        functools.partial(clip_kernel, limit_square),
        out_shape=(
            jax.ShapeDtypeStruct((own_rows, 1, width), F32),
            jax.ShapeDtypeStruct((1, 1), F32),
        ),
        out_specs=(
            pl.BlockSpec(memory_space=pltpu.VMEM),
            pl.BlockSpec(memory_space=pltpu.SMEM),
        ),
        compiler_params=pltpu.CompilerParams(vmem_limit_bytes=12 << 20),
        name="clip",
    )(back, squares)


def body(hidden, projection_weight, norm_gain, upstream, loss_mask):
    tok, joined = hidden.shape
    groups = lax.axis_size(GROUP)
    shard, width = projection_weight.shape
    slices = YS * CORES
    part = width // slices
    own_rows = shard // (ZHI * slices)

    sent = lax.optimization_barrier(hidden.reshape(tok, groups, shard).transpose(1, 0, 2))
    offset = lax.axis_index(GROUP) * tok
    own_cotangent = lax.dynamic_slice_in_dim(upstream, offset, tok, 0)
    own_mask = lax.dynamic_slice_in_dim(loss_mask, offset, tok, 0)
    scaled = norm_gain * (own_cotangent.astype(F32) * own_mask.astype(F32)[:, None])
    columns = exchange(sent, GROUP)
    columns, scaled = lax.optimization_barrier((columns, scaled))
    columns = columns.reshape(groups * tok, shard)
    all_columns = lax.all_gather(columns, ALONG, axis=0, tiled=True)

    partial_value = jnp.dot(columns, projection_weight, preferred_element_type=F32).astype(BF16)
    parts = exchange(lax.optimization_barrier(partial_value.reshape(groups, tok, width)), GROUP)

    cut = exchange(norm_backward(parts, scaled, slices), ALONG)
    spread = lax.optimization_barrier(jnp.broadcast_to(cut[None], (groups, slices, tok, part)))
    arrived = exchange(spread, GROUP)
    block = product(all_columns, arrived, 4)
    by_zh = exchange(block.reshape(ZHI, shard // ZHI, part), "zh")

    back = exchange(gather_rows(by_zh, own_rows, slices, 16), ALONG)
    squares = exchange(spread_squares(back, own_rows, ZHI * groups), ("zh",) + GROUP)
    rows, grad_norm = clip(back, squares, own_rows, width, float(joined * width))
    return (rows.transpose(1, 0, 2), grad_norm.reshape(()))


def solution(mesh):
    sizes = (ZHI, YS, CORES, mesh.shape["blk"], mesh.shape["tp"])
    fine = Mesh(mesh.devices.reshape(sizes), REP + GROUP)
    return jax.shard_map(
        body,
        mesh=fine,
        in_specs=(
            P(REP + GROUP, None),
            P(GROUP, None),
            P(),
            P(REP, None),
            P(REP),
        ),
        out_specs=(P(GROUP, REP, None), P()),
        check_vma=False,
    )
```

```python
import functools

import jax
import jax.numpy as jnp
from jax import lax
from jax.experimental import pallas as pl
from jax.experimental.pallas import tpu as pltpu
from jax.sharding import Mesh, PartitionSpec as P

ZHI, YS, CORES = 4, 8, 2
REP = ("zh", "y", "core")
ALONG = ("y", "core")
GROUP = ("blk", "tp")
LANES = 128
HELD = (-1, 0, 1, -4, -3, -2, 2, 3)
BF16, F32 = jnp.bfloat16, jnp.float32


def exchange(blocks, axes):
    return lax.all_to_all(blocks, axes, split_axis=0, concat_axis=0, tiled=True)


def move(value, step):
    return lax.ppermute(value, "y", [(i, (i + step) % YS) for i in range(YS)])


def norm_backward_kernel(parts_ref, scaled_ref, out_ref):
    groups = parts_ref.shape[0]
    projected = parts_ref[0].astype(F32)
    for g in range(1, groups):
        projected += parts_ref[g].astype(F32)
    scaled = scaled_ref[...]
    inverse_rms = lax.rsqrt(jnp.mean(projected * projected, axis=1, keepdims=True) + 1e-06)
    normed = projected * inverse_rms
    along = jnp.mean(scaled * normed, axis=1, keepdims=True)
    token_grad = (inverse_rms * (scaled - normed * along)).astype(BF16)
    for j in range(out_ref.shape[0]):
        out_ref[j] = token_grad[:, j * LANES : (j + 1) * LANES]


def norm_backward(parts, scaled, slices):
    _, tok, width = parts.shape
    return pl.pallas_call(
        norm_backward_kernel,
        out_shape=jax.ShapeDtypeStruct((slices, tok, width // slices), BF16),
        compiler_params=pltpu.CompilerParams(vmem_limit_bytes=12 << 20),
        name="norm_backward",
    )(parts, scaled)


def product_kernel(own_ref, other_ref, grads_ref, out_ref, total_ref):
    half = pl.program_id(0)
    y, core = lax.axis_index("y"), lax.axis_index("core")
    groups, _, _, tok, part = grads_ref.shape
    count = own_ref.shape[0]
    term = None
    for columns_ref, place in ((own_ref, core), (other_ref, 1 - core)):
        grads = []
        for k in range(count):
            source = lax.rem(y + jnp.where(half == 0, HELD[k], HELD[count + k]) + YS, YS)
            grads.append(grads_ref[:, source, place].astype(F32).reshape(groups * tok, part).T)
        grads = jnp.concatenate(grads, axis=1).astype(BF16)
        columns = columns_ref[...].reshape(-1, columns_ref.shape[2])
        dot = jnp.dot(grads, columns, preferred_element_type=F32)
        term = dot if term is None else term + dot

    @pl.when(half == 0)
    def _():
        total_ref[...] = term

    @pl.when(half == 1)
    def _():
        out_ref[...] = (total_ref[...] + term).T.astype(BF16)


def product(own, other, arrived):
    part = arrived.shape[-1]
    _, tokens, shard = own.shape
    held = pl.BlockSpec((YS // 2, tokens, shard), lambda i: (i, 0, 0))
    return pl.pallas_call(
        product_kernel,
        grid=(2,),
        in_specs=[held, held, pl.BlockSpec(arrived.shape, lambda i: (0, 0, 0, 0, 0))],
        out_specs=pl.BlockSpec((shard, part), lambda i: (0, 0)),
        out_shape=jax.ShapeDtypeStruct((shard, part), BF16),
        scratch_shapes=[pltpu.VMEM((part, shard), F32)],
        name="product",
    )(own, other, arrived)


def gather_rows_kernel(own_rows, pieces_ref, out_ref):
    total = pieces_ref[0].astype(F32)
    for k in range(1, pieces_ref.shape[0]):
        total += pieces_ref[k].astype(F32)
    slices, padded, part = out_ref.shape
    squares = jnp.full((padded - own_rows, part), jnp.sum(total * total), F32)
    for j in range(slices):
        out_ref[j, :own_rows] = total[j * own_rows : (j + 1) * own_rows]
        out_ref[j, own_rows:] = squares


def gather_rows(pieces, own_rows, slices, padded):
    return pl.pallas_call(
        functools.partial(gather_rows_kernel, own_rows),
        out_shape=jax.ShapeDtypeStruct((slices, padded, pieces.shape[2]), F32),
        compiler_params=pltpu.CompilerParams(vmem_limit_bytes=12 << 20),
        name="gather_rows",
    )(pieces)


def squares_kernel(own_rows, back_ref, out_ref):
    total = jnp.sum(back_ref[:, own_rows : own_rows + 1, :], axis=0)
    out_ref[...] = jnp.broadcast_to(total[None], out_ref.shape)


def spread_squares(back, own_rows, size):
    return pl.pallas_call(
        functools.partial(squares_kernel, own_rows),
        out_shape=jax.ShapeDtypeStruct((size, 1, back.shape[2]), F32),
        compiler_params=pltpu.CompilerParams(vmem_limit_bytes=12 << 20),
        name="spread_squares",
    )(back)


def clip_kernel(limit_square, back_ref, squares_ref, out_ref, norm_ref):
    squares = jnp.sum(squares_ref[...], axis=0)
    norm = jnp.sqrt(squares)
    factor = jnp.minimum(1.0, jnp.sqrt(jnp.full_like(norm, limit_square)) / (norm + 1e-06))
    norm_ref[0, 0] = jnp.max(norm)
    slices, _, part = back_ref.shape
    for j in range(slices):
        for r in range(out_ref.shape[0]):
            out_ref[r, :, j * part : (j + 1) * part] = back_ref[j, r : r + 1, :] * factor


def clip(back, squares, own_rows, width, limit_square):
    return pl.pallas_call(
        functools.partial(clip_kernel, limit_square),
        out_shape=(
            jax.ShapeDtypeStruct((own_rows, 1, width), F32),
            jax.ShapeDtypeStruct((1, 1), F32),
        ),
        out_specs=(
            pl.BlockSpec(memory_space=pltpu.VMEM),
            pl.BlockSpec(memory_space=pltpu.SMEM),
        ),
        compiler_params=pltpu.CompilerParams(vmem_limit_bytes=12 << 20),
        name="clip",
    )(back, squares)


def body(hidden, projection_weight, norm_gain, upstream, loss_mask):
    tok, joined = hidden.shape
    groups = lax.axis_size(GROUP)
    shard, width = projection_weight.shape
    slices = YS * CORES
    part = width // slices
    own_rows = shard // (ZHI * slices)

    sent = lax.optimization_barrier(hidden.reshape(tok, groups, shard).transpose(1, 0, 2))
    offset = lax.axis_index(GROUP) * tok
    own_cotangent = lax.dynamic_slice_in_dim(upstream, offset, tok, 0)
    own_mask = lax.dynamic_slice_in_dim(loss_mask, offset, tok, 0)
    scaled = norm_gain * (own_cotangent.astype(F32) * own_mask.astype(F32)[:, None])
    columns = exchange(sent, GROUP)
    columns, scaled = lax.optimization_barrier((columns, scaled))
    columns = columns.reshape(groups * tok, shard)
    up, down = move(columns, 1), move(columns, -1)
    three = jnp.stack([up, columns, down])
    own = jnp.concatenate([three, move(three, 3), move(three[:2], -3)])
    other = lax.ppermute(own, "core", [(0, 1), (1, 0)])

    partial_value = jnp.dot(columns, projection_weight, preferred_element_type=F32).astype(BF16)
    parts = exchange(lax.optimization_barrier(partial_value.reshape(groups, tok, width)), GROUP)

    cut = exchange(norm_backward(parts, scaled, slices), ALONG)
    spread = lax.optimization_barrier(jnp.broadcast_to(cut[None], (groups, slices, tok, part)))
    arrived = exchange(spread, GROUP)
    block = product(own, other, arrived.reshape(groups, YS, CORES, tok, part))
    by_zh = exchange(block.reshape(ZHI, shard // ZHI, part), "zh")

    back = exchange(gather_rows(by_zh, own_rows, slices, 16), ALONG)
    squares = exchange(spread_squares(back, own_rows, ZHI * groups), ("zh",) + GROUP)
    rows, grad_norm = clip(back, squares, own_rows, width, float(joined * width))
    return (rows.transpose(1, 0, 2), grad_norm.reshape(()))


def solution(mesh):
    sizes = (ZHI, YS, CORES, mesh.shape["blk"], mesh.shape["tp"])
    fine = Mesh(mesh.devices.reshape(sizes), REP + GROUP)
    return jax.shard_map(
        body,
        mesh=fine,
        in_specs=(
            P(REP + GROUP, None),
            P(GROUP, None),
            P(),
            P(REP, None),
            P(REP),
        ),
        out_specs=(P(GROUP, REP, None), P()),
        check_vma=False,
    )
```

```python
import functools

import jax
import jax.numpy as jnp
from jax import lax
from jax.experimental import pallas as pl
from jax.experimental.pallas import tpu as pltpu
from jax.sharding import Mesh, PartitionSpec as P

ZHI, YS, CORES = 4, 8, 2
REP = ("zh", "y", "core")
ALONG = ("y", "core")
GROUP = ("blk", "tp")
LANES = 128
BF16, F32 = jnp.bfloat16, jnp.float32


def exchange(blocks, axes):
    return lax.all_to_all(blocks, axes, split_axis=0, concat_axis=0, tiled=True)


def norm_backward_kernel(parts_ref, scaled_ref, out_ref):
    groups = parts_ref.shape[0]
    projected = parts_ref[0].astype(F32)
    for g in range(1, groups):
        projected += parts_ref[g].astype(F32)
    scaled = scaled_ref[...]
    inverse_rms = lax.rsqrt(jnp.mean(projected * projected, axis=1, keepdims=True) + 1e-06)
    normed = projected * inverse_rms
    along = jnp.mean(scaled * normed, axis=1, keepdims=True)
    token_grad = (inverse_rms * (scaled - normed * along)).astype(BF16)
    for j in range(out_ref.shape[0]):
        out_ref[j] = token_grad[:, j * LANES : (j + 1) * LANES]


def norm_backward(parts, scaled, slices):
    _, tok, width = parts.shape
    return pl.pallas_call(
        norm_backward_kernel,
        out_shape=jax.ShapeDtypeStruct((slices, tok, width // slices), BF16),
        compiler_params=pltpu.CompilerParams(vmem_limit_bytes=12 << 20),
        name="norm_backward",
    )(parts, scaled)


def product_kernel(columns_ref, grads_ref, out_ref, total_ref):
    step = pl.program_id(0)

    @pl.when(step == 0)
    def _():
        total_ref[...] = jnp.zeros_like(total_ref)

    groups, chunk, tok, part = grads_ref.shape
    grads = grads_ref[...].astype(F32).transpose(1, 0, 2, 3).reshape(chunk * groups * tok, part)
    total_ref[...] += jnp.dot(grads.T.astype(BF16), columns_ref[...], preferred_element_type=F32)

    @pl.when(step == pl.num_programs(0) - 1)
    def _():
        out_ref[...] = total_ref[...].T.astype(BF16)


def product(all_columns, arrived, steps):
    groups, slices, tok, part = arrived.shape
    tokens, shard = all_columns.shape
    return pl.pallas_call(
        product_kernel,
        grid=(steps,),
        in_specs=[
            pl.BlockSpec((tokens // steps, shard), lambda i: (i, 0)),
            pl.BlockSpec((groups, slices // steps, tok, part), lambda i: (0, i, 0, 0)),
        ],
        out_specs=pl.BlockSpec((shard, part), lambda i: (0, 0)),
        out_shape=jax.ShapeDtypeStruct((shard, part), BF16),
        scratch_shapes=[pltpu.VMEM((part, shard), F32)],
        name="product",
    )(all_columns, arrived)


def gather_rows_kernel(own_rows, pieces_ref, out_ref):
    total = pieces_ref[0].astype(F32)
    for k in range(1, pieces_ref.shape[0]):
        total += pieces_ref[k].astype(F32)
    slices, padded, part = out_ref.shape
    squares = jnp.full((padded - own_rows, part), jnp.sum(total * total), F32)
    for j in range(slices):
        out_ref[j, :own_rows] = total[j * own_rows : (j + 1) * own_rows]
        out_ref[j, own_rows:] = squares


def gather_rows(pieces, own_rows, slices, padded):
    return pl.pallas_call(
        functools.partial(gather_rows_kernel, own_rows),
        out_shape=jax.ShapeDtypeStruct((slices, padded, pieces.shape[2]), F32),
        compiler_params=pltpu.CompilerParams(vmem_limit_bytes=12 << 20),
        name="gather_rows",
    )(pieces)


def squares_kernel(own_rows, back_ref, out_ref):
    total = jnp.sum(back_ref[:, own_rows : own_rows + 1, :], axis=0)
    out_ref[...] = jnp.broadcast_to(total[None], out_ref.shape)


def spread_squares(back, own_rows, size):
    return pl.pallas_call(
        functools.partial(squares_kernel, own_rows),
        out_shape=jax.ShapeDtypeStruct((size, 1, back.shape[2]), F32),
        compiler_params=pltpu.CompilerParams(vmem_limit_bytes=12 << 20),
        name="spread_squares",
    )(back)


def clip_kernel(limit_square, back_ref, squares_ref, out_ref, norm_ref):
    squares = jnp.sum(squares_ref[...], axis=0)
    norm = jnp.sqrt(squares)
    factor = jnp.minimum(1.0, jnp.sqrt(jnp.full_like(norm, limit_square)) / (norm + 1e-06))
    norm_ref[0, 0] = jnp.max(norm)
    slices, _, part = back_ref.shape
    for j in range(slices):
        for r in range(out_ref.shape[0]):
            out_ref[r, :, j * part : (j + 1) * part] = back_ref[j, r : r + 1, :] * factor


def clip(back, squares, own_rows, width, limit_square):
    return pl.pallas_call(
        functools.partial(clip_kernel, limit_square),
        out_shape=(
            jax.ShapeDtypeStruct((own_rows, 1, width), F32),
            jax.ShapeDtypeStruct((1, 1), F32),
        ),
        out_specs=(
            pl.BlockSpec(memory_space=pltpu.VMEM),
            pl.BlockSpec(memory_space=pltpu.SMEM),
        ),
        compiler_params=pltpu.CompilerParams(vmem_limit_bytes=12 << 20),
        name="clip",
    )(back, squares)


def body(hidden, projection_weight, norm_gain, upstream, loss_mask):
    tok, joined = hidden.shape
    groups = lax.axis_size(GROUP)
    shard, width = projection_weight.shape
    slices = YS * CORES
    part = width // slices
    own_rows = shard // (ZHI * slices)

    sent = lax.optimization_barrier(hidden.reshape(tok, groups, shard).transpose(1, 0, 2))
    offset = lax.axis_index(GROUP) * tok
    own_cotangent = lax.dynamic_slice_in_dim(upstream, offset, tok, 0)
    own_mask = lax.dynamic_slice_in_dim(loss_mask, offset, tok, 0)
    scaled = norm_gain * (own_cotangent.astype(F32) * own_mask.astype(F32)[:, None])
    columns = exchange(sent, GROUP)
    columns, scaled = lax.optimization_barrier((columns, scaled))
    columns = columns.reshape(groups * tok, shard)
    all_columns = lax.all_gather(columns, ALONG, axis=0, tiled=True)

    partial_value = jnp.dot(columns, projection_weight, preferred_element_type=F32).astype(BF16)
    parts = exchange(lax.optimization_barrier(partial_value.reshape(groups, tok, width)), GROUP)

    cut = exchange(norm_backward(parts, scaled, slices), ALONG)
    spread = lax.optimization_barrier(jnp.broadcast_to(cut[None], (groups, slices, tok, part)))
    arrived = exchange(spread, GROUP)
    block = product(all_columns, arrived, 2)
    by_zh = exchange(block.reshape(ZHI, shard // ZHI, part), "zh")

    back = exchange(gather_rows(by_zh, own_rows, slices, 16), ALONG)
    squares = exchange(spread_squares(back, own_rows, ZHI * groups), ("zh",) + GROUP)
    rows, grad_norm = clip(back, squares, own_rows, width, float(joined * width))
    return (rows.transpose(1, 0, 2), grad_norm.reshape(()))


def solution(mesh):
    sizes = (ZHI, YS, CORES, mesh.shape["blk"], mesh.shape["tp"])
    fine = Mesh(mesh.devices.reshape(sizes), REP + GROUP)
    return jax.shard_map(
        body,
        mesh=fine,
        in_specs=(
            P(REP + GROUP, None),
            P(GROUP, None),
            P(),
            P(REP, None),
            P(REP),
        ),
        out_specs=(P(GROUP, REP, None), P()),
        check_vma=False,
    )
```

```python
import functools

import jax
import jax.numpy as jnp
from jax import lax
from jax.experimental import pallas as pl
from jax.experimental.pallas import tpu as pltpu
from jax.sharding import Mesh, PartitionSpec as P

ZHI, YS, CORES, HALVES = 4, 8, 2, 2
REP = ("zh", "y", "core")
ALONG = ("y", "core")
GROUP = ("blk", "ta", "tb")
PAIR = [(0, 1), (1, 0)]
LANES = 128
BF16, F32 = jnp.bfloat16, jnp.float32


def exchange(blocks, axes):
    return lax.all_to_all(blocks, axes, split_axis=0, concat_axis=0, tiled=True)


def norm_backward_kernel(parts_ref, scaled_ref, out_ref):
    groups = parts_ref.shape[0]
    projected = parts_ref[0].astype(F32)
    for g in range(1, groups):
        projected += parts_ref[g].astype(F32)
    scaled = scaled_ref[...]
    inverse_rms = lax.rsqrt(jnp.mean(projected * projected, axis=1, keepdims=True) + 1e-06)
    normed = projected * inverse_rms
    along = jnp.mean(scaled * normed, axis=1, keepdims=True)
    token_grad = (inverse_rms * (scaled - normed * along)).astype(BF16)
    for j in range(out_ref.shape[0]):
        out_ref[j] = token_grad[:, j * LANES : (j + 1) * LANES]


def norm_backward(parts, scaled, slices):
    _, tok, width = parts.shape
    return pl.pallas_call(
        norm_backward_kernel,
        out_shape=jax.ShapeDtypeStruct((slices, tok, width // slices), BF16),
        compiler_params=pltpu.CompilerParams(vmem_limit_bytes=12 << 20),
        name="norm_backward",
    )(parts, scaled)


def product_kernel(columns_ref, grads_ref, out_ref, total_ref):
    step = pl.program_id(0)

    @pl.when(step == 0)
    def _():
        total_ref[...] = jnp.zeros_like(total_ref)

    groups, chunk, tok, part = grads_ref.shape
    grads = grads_ref[...].astype(F32).transpose(1, 0, 2, 3).reshape(chunk * groups * tok, part)
    total_ref[...] += jnp.dot(grads.T.astype(BF16), columns_ref[...], preferred_element_type=F32)

    @pl.when(step == pl.num_programs(0) - 1)
    def _():
        out_ref[...] = total_ref[...].T.astype(BF16)


def product(all_columns, arrived, steps):
    groups, slices, tok, part = arrived.shape
    tokens, shard = all_columns.shape
    return pl.pallas_call(
        product_kernel,
        grid=(steps,),
        in_specs=[
            pl.BlockSpec((tokens // steps, shard), lambda i: (i, 0)),
            pl.BlockSpec((groups, slices // steps, tok, part), lambda i: (0, i, 0, 0)),
        ],
        out_specs=pl.BlockSpec((shard, part), lambda i: (0, 0)),
        out_shape=jax.ShapeDtypeStruct((shard, part), BF16),
        scratch_shapes=[pltpu.VMEM((part, shard), F32)],
        name="product",
    )(all_columns, arrived)


def gather_rows_kernel(own_rows, pieces_ref, out_ref):
    total = pieces_ref[0].astype(F32)
    for k in range(1, pieces_ref.shape[0]):
        total += pieces_ref[k].astype(F32)
    slices, padded, part = out_ref.shape
    squares = jnp.full((padded - own_rows, part), jnp.sum(total * total), F32)
    for j in range(slices):
        out_ref[j, :own_rows] = total[j * own_rows : (j + 1) * own_rows]
        out_ref[j, own_rows:] = squares


def gather_rows(pieces, own_rows, slices, padded):
    return pl.pallas_call(
        functools.partial(gather_rows_kernel, own_rows),
        out_shape=jax.ShapeDtypeStruct((slices, padded, pieces.shape[2]), F32),
        compiler_params=pltpu.CompilerParams(vmem_limit_bytes=12 << 20),
        name="gather_rows",
    )(pieces)


def squares_kernel(own_rows, back_ref, out_ref):
    total = jnp.sum(back_ref[:, own_rows : own_rows + 1, :], axis=0)
    out_ref[...] = jnp.broadcast_to(total[None], out_ref.shape)


def spread_squares(back, own_rows, size):
    return pl.pallas_call(
        functools.partial(squares_kernel, own_rows),
        out_shape=jax.ShapeDtypeStruct((size, 1, back.shape[2]), F32),
        compiler_params=pltpu.CompilerParams(vmem_limit_bytes=12 << 20),
        name="spread_squares",
    )(back)


def add_squares_kernel(squares_ref, out_ref):
    out_ref[...] = jnp.sum(squares_ref[...], axis=0)


def add_squares(squares):
    return pl.pallas_call(
        add_squares_kernel,
        out_shape=jax.ShapeDtypeStruct(squares.shape[1:], F32),
        compiler_params=pltpu.CompilerParams(vmem_limit_bytes=12 << 20),
        name="add_squares",
    )(squares)


def clip_kernel(limit_square, back_ref, squares_ref, other_ref, out_ref, norm_ref):
    norm = jnp.sqrt(squares_ref[...] + other_ref[...])
    factor = jnp.minimum(1.0, jnp.sqrt(jnp.full_like(norm, limit_square)) / (norm + 1e-06))
    norm_ref[0, 0] = jnp.max(norm)
    slices, _, part = back_ref.shape
    for j in range(slices):
        for r in range(out_ref.shape[0]):
            out_ref[r, :, j * part : (j + 1) * part] = back_ref[j, r : r + 1, :] * factor


def clip(back, squares, other, own_rows, width, limit_square):
    return pl.pallas_call(
        functools.partial(clip_kernel, limit_square),
        out_shape=(
            jax.ShapeDtypeStruct((own_rows, 1, width), F32),
            jax.ShapeDtypeStruct((1, 1), F32),
        ),
        out_specs=(
            pl.BlockSpec(memory_space=pltpu.VMEM),
            pl.BlockSpec(memory_space=pltpu.SMEM),
        ),
        compiler_params=pltpu.CompilerParams(vmem_limit_bytes=12 << 20),
        name="clip",
    )(back, squares, other)


def body(hidden, projection_weight, norm_gain, upstream, loss_mask):
    tok, joined = hidden.shape
    groups = lax.axis_size(GROUP)
    shard, width = projection_weight.shape
    slices = YS * CORES
    part = width // slices
    own_rows = shard // (ZHI * slices)

    sent = lax.optimization_barrier(hidden.reshape(tok, groups, shard).transpose(1, 0, 2))
    offset = lax.axis_index(GROUP) * tok
    own_cotangent = lax.dynamic_slice_in_dim(upstream, offset, tok, 0)
    own_mask = lax.dynamic_slice_in_dim(loss_mask, offset, tok, 0)
    scaled = norm_gain * (own_cotangent.astype(F32) * own_mask.astype(F32)[:, None])
    columns = exchange(sent, GROUP)
    columns, scaled = lax.optimization_barrier((columns, scaled))
    columns = columns.reshape(groups * tok, shard)
    partial_value = jnp.dot(columns, projection_weight, preferred_element_type=F32).astype(BF16)
    columns, partial_value = lax.optimization_barrier((columns, partial_value))
    all_columns = lax.all_gather(columns, ALONG, axis=0, tiled=True)
    parts = exchange(lax.optimization_barrier(partial_value.reshape(groups, tok, width)), GROUP)

    cut = exchange(norm_backward(parts, scaled, slices), ALONG)
    spread = lax.optimization_barrier(jnp.broadcast_to(cut[None], (groups, slices, tok, part)))
    arrived = exchange(spread, GROUP)
    block = product(all_columns, arrived, 2)
    by_zh = exchange(block.reshape(ZHI, shard // ZHI, part), "zh")

    back = exchange(gather_rows(by_zh, own_rows, slices, 16), ALONG)
    squares = spread_squares(back, own_rows, ZHI * groups // HALVES)
    squares = add_squares(exchange(squares, ("zh", "blk", "ta")))
    other = lax.ppermute(squares, "tb", PAIR)
    rows, grad_norm = clip(back, squares, other, own_rows, width, float(joined * width))
    return (rows.transpose(1, 0, 2), grad_norm.reshape(()))


def solution(mesh):
    sizes = (ZHI, YS, CORES, mesh.shape["blk"], mesh.shape["tp"] // HALVES, HALVES)
    fine = Mesh(mesh.devices.reshape(sizes), REP + GROUP)
    return jax.shard_map(
        body,
        mesh=fine,
        in_specs=(
            P(REP + GROUP, None),
            P(GROUP, None),
            P(),
            P(REP, None),
            P(REP),
        ),
        out_specs=(P(GROUP, REP, None), P()),
        check_vma=False,
    )
```

```python
import functools

import jax
import jax.numpy as jnp
from jax import lax
from jax.experimental import pallas as pl
from jax.experimental.pallas import tpu as pltpu
from jax.sharding import Mesh, PartitionSpec as P

ZHI, YS, CORES = 4, 8, 2
REP = ("zh", "y", "core")
ALONG = ("y", "core")
GROUP = ("blk", "tp")
LANES = 128
BF16, F32 = jnp.bfloat16, jnp.float32


def exchange(blocks, axes):
    return lax.all_to_all(blocks, axes, split_axis=0, concat_axis=0, tiled=True)


def norm_backward_kernel(parts_ref, scaled_ref, out_ref):
    groups = parts_ref.shape[0]
    projected = parts_ref[0].astype(F32)
    for g in range(1, groups):
        projected += parts_ref[g].astype(F32)
    scaled = scaled_ref[...]
    inverse_rms = lax.rsqrt(jnp.mean(projected * projected, axis=1, keepdims=True) + 1e-06)
    normed = projected * inverse_rms
    along = jnp.mean(scaled * normed, axis=1, keepdims=True)
    token_grad = (inverse_rms * (scaled - normed * along)).astype(BF16)
    for j in range(out_ref.shape[0]):
        out_ref[j] = token_grad[:, j * LANES : (j + 1) * LANES]


def norm_backward(parts, scaled, slices):
    _, tok, width = parts.shape
    return pl.pallas_call(
        norm_backward_kernel,
        out_shape=jax.ShapeDtypeStruct((slices, tok, width // slices), BF16),
        compiler_params=pltpu.CompilerParams(vmem_limit_bytes=12 << 20),
        name="norm_backward",
    )(parts, scaled)


def product_kernel(columns_ref, grads_ref, out_ref, total_ref):
    step = pl.program_id(0)

    @pl.when(step == 0)
    def _():
        total_ref[...] = jnp.zeros_like(total_ref)

    groups, chunk, tok, part = grads_ref.shape
    grads = grads_ref[...].astype(F32).transpose(1, 0, 2, 3).reshape(chunk * groups * tok, part)
    total_ref[...] += jnp.dot(grads.T.astype(BF16), columns_ref[...], preferred_element_type=F32)

    @pl.when(step == pl.num_programs(0) - 1)
    def _():
        out_ref[...] = total_ref[...].T.astype(BF16)


def product(all_columns, arrived, steps):
    groups, slices, tok, part = arrived.shape
    tokens, shard = all_columns.shape
    return pl.pallas_call(
        product_kernel,
        grid=(steps,),
        in_specs=[
            pl.BlockSpec((tokens // steps, shard), lambda i: (i, 0)),
            pl.BlockSpec((groups, slices // steps, tok, part), lambda i: (0, i, 0, 0)),
        ],
        out_specs=pl.BlockSpec((shard, part), lambda i: (0, 0)),
        out_shape=jax.ShapeDtypeStruct((shard, part), BF16),
        scratch_shapes=[pltpu.VMEM((part, shard), F32)],
        compiler_params=pltpu.CompilerParams(vmem_limit_bytes=53 << 20),
        name="product",
    )(all_columns, arrived)


def gather_rows_kernel(own_rows, pieces_ref, out_ref):
    total = pieces_ref[0].astype(F32)
    for k in range(1, pieces_ref.shape[0]):
        total += pieces_ref[k].astype(F32)
    slices, padded, part = out_ref.shape
    squares = jnp.full((padded - own_rows, part), jnp.sum(total * total), F32)
    for j in range(slices):
        out_ref[j, :own_rows] = total[j * own_rows : (j + 1) * own_rows]
        out_ref[j, own_rows:] = squares


def gather_rows(pieces, own_rows, slices, padded):
    return pl.pallas_call(
        functools.partial(gather_rows_kernel, own_rows),
        out_shape=jax.ShapeDtypeStruct((slices, padded, pieces.shape[2]), F32),
        compiler_params=pltpu.CompilerParams(vmem_limit_bytes=12 << 20),
        name="gather_rows",
    )(pieces)


def squares_kernel(own_rows, back_ref, out_ref):
    total = jnp.sum(back_ref[:, own_rows : own_rows + 1, :], axis=0)
    out_ref[...] = jnp.broadcast_to(total[None], out_ref.shape)


def spread_squares(back, own_rows, size):
    return pl.pallas_call(
        functools.partial(squares_kernel, own_rows),
        out_shape=jax.ShapeDtypeStruct((size, 1, back.shape[2]), F32),
        compiler_params=pltpu.CompilerParams(vmem_limit_bytes=12 << 20),
        name="spread_squares",
    )(back)


def clip_kernel(limit_square, back_ref, squares_ref, out_ref, norm_ref):
    squares = jnp.sum(squares_ref[...], axis=0)
    norm = jnp.sqrt(squares)
    factor = jnp.minimum(1.0, jnp.sqrt(jnp.full_like(norm, limit_square)) / (norm + 1e-06))
    norm_ref[0, 0] = jnp.max(norm)
    slices, _, part = back_ref.shape
    for j in range(slices):
        for r in range(out_ref.shape[0]):
            out_ref[r, :, j * part : (j + 1) * part] = back_ref[j, r : r + 1, :] * factor


def clip(back, squares, own_rows, width, limit_square):
    return pl.pallas_call(
        functools.partial(clip_kernel, limit_square),
        out_shape=(
            jax.ShapeDtypeStruct((own_rows, 1, width), F32),
            jax.ShapeDtypeStruct((1, 1), F32),
        ),
        out_specs=(
            pl.BlockSpec(memory_space=pltpu.VMEM),
            pl.BlockSpec(memory_space=pltpu.SMEM),
        ),
        compiler_params=pltpu.CompilerParams(vmem_limit_bytes=12 << 20),
        name="clip",
    )(back, squares)


def body(hidden, projection_weight, norm_gain, upstream, loss_mask):
    tok, joined = hidden.shape
    groups = lax.axis_size(GROUP)
    shard, width = projection_weight.shape
    slices = YS * CORES
    part = width // slices
    own_rows = shard // (ZHI * slices)

    sent = lax.optimization_barrier(hidden.reshape(tok, groups, shard).transpose(1, 0, 2))
    offset = lax.axis_index(GROUP) * tok
    own_cotangent = lax.dynamic_slice_in_dim(upstream, offset, tok, 0)
    own_mask = lax.dynamic_slice_in_dim(loss_mask, offset, tok, 0)
    scaled = norm_gain * (own_cotangent.astype(F32) * own_mask.astype(F32)[:, None])
    columns = exchange(sent, GROUP)
    columns, scaled = lax.optimization_barrier((columns, scaled))
    columns = columns.reshape(groups * tok, shard)
    partial_value = jnp.dot(columns, projection_weight, preferred_element_type=F32).astype(BF16)
    columns, partial_value = lax.optimization_barrier((columns, partial_value))
    all_columns = lax.all_gather(columns, ALONG, axis=0, tiled=True)
    parts = exchange(lax.optimization_barrier(partial_value.reshape(groups, tok, width)), GROUP)

    cut = exchange(norm_backward(parts, scaled, slices), ALONG)
    spread = lax.optimization_barrier(jnp.broadcast_to(cut[None], (groups, slices, tok, part)))
    arrived = exchange(spread, GROUP)
    block = product(all_columns, arrived, 2)
    by_zh = exchange(block.reshape(ZHI, shard // ZHI, part), "zh")

    back = exchange(gather_rows(by_zh, own_rows, slices, 16), ALONG)
    squares = exchange(spread_squares(back, own_rows, ZHI * groups), ("zh",) + GROUP)
    rows, grad_norm = clip(back, squares, own_rows, width, float(joined * width))
    return (rows.transpose(1, 0, 2), grad_norm.reshape(()))


def solution(mesh):
    sizes = (ZHI, YS, CORES, mesh.shape["blk"], mesh.shape["tp"])
    fine = Mesh(mesh.devices.reshape(sizes), REP + GROUP)
    return jax.shard_map(
        body,
        mesh=fine,
        in_specs=(
            P(REP + GROUP, None),
            P(GROUP, None),
            P(),
            P(REP, None),
            P(REP),
        ),
        out_specs=(P(GROUP, REP, None), P()),
        check_vma=False,
    )
```

```python
import functools

import jax
import jax.numpy as jnp
from jax import lax
from jax.experimental import pallas as pl
from jax.experimental.pallas import tpu as pltpu
from jax.sharding import Mesh, PartitionSpec as P

ZHI, YS, CORES = 4, 8, 2
REP = ("zh", "y", "core")
ALONG = ("y", "core")
GROUP = ("blk", "tp")
LANES = 128
BF16, F32 = jnp.bfloat16, jnp.float32


def exchange(blocks, axes):
    return lax.all_to_all(blocks, axes, split_axis=0, concat_axis=0, tiled=True)


def norm_backward_kernel(parts_ref, scaled_ref, out_ref):
    groups = parts_ref.shape[0]
    projected = parts_ref[0].astype(F32)
    for g in range(1, groups):
        projected += parts_ref[g].astype(F32)
    scaled = scaled_ref[...]
    inverse_rms = lax.rsqrt(jnp.mean(projected * projected, axis=1, keepdims=True) + 1e-06)
    normed = projected * inverse_rms
    along = jnp.mean(scaled * normed, axis=1, keepdims=True)
    token_grad = (inverse_rms * (scaled - normed * along)).astype(BF16)
    for j in range(out_ref.shape[0]):
        out_ref[j] = token_grad[:, j * LANES : (j + 1) * LANES]


def norm_backward(parts, scaled, slices):
    _, tok, width = parts.shape
    return pl.pallas_call(
        norm_backward_kernel,
        out_shape=jax.ShapeDtypeStruct((slices, tok, width // slices), BF16),
        compiler_params=pltpu.CompilerParams(vmem_limit_bytes=12 << 20),
        name="norm_backward",
    )(parts, scaled)


def product_kernel(columns_ref, grads_ref, out_ref, total_ref):
    step = pl.program_id(0)

    @pl.when(step == 0)
    def _():
        total_ref[...] = jnp.zeros_like(total_ref)

    groups, chunk, tok, part = grads_ref.shape
    grads = grads_ref[...].astype(F32).transpose(1, 0, 2, 3).reshape(chunk * groups * tok, part)
    total_ref[...] += jnp.dot(grads.T.astype(BF16), columns_ref[...], preferred_element_type=F32)

    @pl.when(step == pl.num_programs(0) - 1)
    def _():
        out_ref[...] = total_ref[...].T.astype(BF16)


def product(all_columns, arrived, steps):
    groups, slices, tok, part = arrived.shape
    tokens, shard = all_columns.shape
    return pl.pallas_call(
        product_kernel,
        grid=(steps,),
        in_specs=[
            pl.BlockSpec((tokens // steps, shard), lambda i: (i, 0)),
            pl.BlockSpec((groups, slices // steps, tok, part), lambda i: (0, i, 0, 0)),
        ],
        out_specs=pl.BlockSpec((shard, part), lambda i: (0, 0)),
        out_shape=jax.ShapeDtypeStruct((shard, part), BF16),
        scratch_shapes=[pltpu.VMEM((part, shard), F32)],
        compiler_params=pltpu.CompilerParams(vmem_limit_bytes=55040 << 10),
        name="product",
    )(all_columns, arrived)


def gather_rows_kernel(own_rows, pieces_ref, out_ref):
    total = pieces_ref[0].astype(F32)
    for k in range(1, pieces_ref.shape[0]):
        total += pieces_ref[k].astype(F32)
    slices, padded, part = out_ref.shape
    squares = jnp.full((padded - own_rows, part), jnp.sum(total * total), F32)
    for j in range(slices):
        out_ref[j, :own_rows] = total[j * own_rows : (j + 1) * own_rows]
        out_ref[j, own_rows:] = squares


def gather_rows(pieces, own_rows, slices, padded):
    return pl.pallas_call(
        functools.partial(gather_rows_kernel, own_rows),
        out_shape=jax.ShapeDtypeStruct((slices, padded, pieces.shape[2]), F32),
        compiler_params=pltpu.CompilerParams(vmem_limit_bytes=12 << 20),
        name="gather_rows",
    )(pieces)


def squares_kernel(own_rows, back_ref, out_ref):
    total = jnp.sum(back_ref[:, own_rows : own_rows + 1, :], axis=0)
    out_ref[...] = jnp.broadcast_to(total[None], out_ref.shape)


def spread_squares(back, own_rows, size):
    return pl.pallas_call(
        functools.partial(squares_kernel, own_rows),
        out_shape=jax.ShapeDtypeStruct((size, 1, back.shape[2]), F32),
        compiler_params=pltpu.CompilerParams(vmem_limit_bytes=12 << 20),
        name="spread_squares",
    )(back)


def clip_kernel(limit_square, back_ref, squares_ref, out_ref, norm_ref):
    squares = jnp.sum(squares_ref[...], axis=0)
    norm = jnp.sqrt(squares)
    factor = jnp.minimum(1.0, jnp.sqrt(jnp.full_like(norm, limit_square)) / (norm + 1e-06))
    norm_ref[0, 0] = jnp.max(norm)
    slices, _, part = back_ref.shape
    for j in range(slices):
        for r in range(out_ref.shape[0]):
            out_ref[r, :, j * part : (j + 1) * part] = back_ref[j, r : r + 1, :] * factor


def clip(back, squares, own_rows, width, limit_square):
    return pl.pallas_call(
        functools.partial(clip_kernel, limit_square),
        out_shape=(
            jax.ShapeDtypeStruct((own_rows, 1, width), F32),
            jax.ShapeDtypeStruct((1, 1), F32),
        ),
        out_specs=(
            pl.BlockSpec(memory_space=pltpu.VMEM),
            pl.BlockSpec(memory_space=pltpu.SMEM),
        ),
        compiler_params=pltpu.CompilerParams(vmem_limit_bytes=12 << 20),
        name="clip",
    )(back, squares)


def body(hidden, projection_weight, norm_gain, upstream, loss_mask):
    tok, joined = hidden.shape
    groups = lax.axis_size(GROUP)
    shard, width = projection_weight.shape
    slices = YS * CORES
    part = width // slices
    own_rows = shard // (ZHI * slices)

    sent = lax.optimization_barrier(hidden.reshape(tok, groups, shard).transpose(1, 0, 2))
    offset = lax.axis_index(GROUP) * tok
    own_cotangent = lax.dynamic_slice_in_dim(upstream, offset, tok, 0)
    own_mask = lax.dynamic_slice_in_dim(loss_mask, offset, tok, 0)
    scaled = norm_gain * (own_cotangent.astype(F32) * own_mask.astype(F32)[:, None])
    columns = exchange(sent, GROUP)
    columns, scaled = lax.optimization_barrier((columns, scaled))
    columns = columns.reshape(groups * tok, shard)
    partial_value = jnp.dot(columns, projection_weight, preferred_element_type=F32).astype(BF16)
    columns, partial_value = lax.optimization_barrier((columns, partial_value))
    all_columns = lax.all_gather(columns, ALONG, axis=0, tiled=True)
    parts = exchange(lax.optimization_barrier(partial_value.reshape(groups, tok, width)), GROUP)

    cut = exchange(norm_backward(parts, scaled, slices), ALONG)
    spread = lax.optimization_barrier(jnp.broadcast_to(cut[None], (groups, slices, tok, part)))
    arrived = exchange(spread, GROUP)
    block = product(all_columns, arrived, 2)
    by_zh = exchange(block.reshape(ZHI, shard // ZHI, part), "zh")

    back = exchange(gather_rows(by_zh, own_rows, slices, 16), ALONG)
    squares = exchange(spread_squares(back, own_rows, ZHI * groups), ("zh",) + GROUP)
    rows, grad_norm = clip(back, squares, own_rows, width, float(joined * width))
    return (rows.transpose(1, 0, 2), grad_norm.reshape(()))


def solution(mesh):
    sizes = (ZHI, YS, CORES, mesh.shape["blk"], mesh.shape["tp"])
    fine = Mesh(mesh.devices.reshape(sizes), REP + GROUP)
    return jax.shard_map(
        body,
        mesh=fine,
        in_specs=(
            P(REP + GROUP, None),
            P(GROUP, None),
            P(),
            P(REP, None),
            P(REP),
        ),
        out_specs=(P(GROUP, REP, None), P()),
        check_vma=False,
    )
```

```python
import functools

import jax
import jax.numpy as jnp
from jax import lax
from jax.experimental import pallas as pl
from jax.experimental.pallas import tpu as pltpu
from jax.sharding import Mesh, PartitionSpec as P

ZHI, YS, CORES = 4, 8, 2
REP = ("zh", "y", "core")
ALONG = ("y", "core")
GROUP = ("blk", "tp")
LANES = 128
BF16, F32 = jnp.bfloat16, jnp.float32


def exchange(blocks, axes):
    return lax.all_to_all(blocks, axes, split_axis=0, concat_axis=0, tiled=True)


def norm_backward_kernel(parts_ref, scaled_ref, out_ref):
    groups = parts_ref.shape[0]
    projected = parts_ref[0].astype(F32)
    for g in range(1, groups):
        projected += parts_ref[g].astype(F32)
    scaled = scaled_ref[...]
    inverse_rms = lax.rsqrt(jnp.mean(projected * projected, axis=1, keepdims=True) + 1e-06)
    normed = projected * inverse_rms
    along = jnp.mean(scaled * normed, axis=1, keepdims=True)
    token_grad = (inverse_rms * (scaled - normed * along)).astype(BF16)
    for j in range(out_ref.shape[0]):
        for k in range(out_ref.shape[1]):
            out_ref[j, k] = token_grad[:, j * LANES : (j + 1) * LANES]


def norm_backward(parts, scaled, slices, copies):
    _, tok, width = parts.shape
    return pl.pallas_call(
        norm_backward_kernel,
        out_shape=jax.ShapeDtypeStruct((slices, copies, tok, width // slices), BF16),
        compiler_params=pltpu.CompilerParams(vmem_limit_bytes=12 << 20),
        name="norm_backward",
    )(parts, scaled)


def product_kernel(columns_ref, grads_ref, out_ref, total_ref):
    step = pl.program_id(0)

    @pl.when(step == 0)
    def _():
        total_ref[...] = jnp.zeros_like(total_ref)

    blks, chunk, tps, tok, part = grads_ref.shape
    grads = grads_ref[...].astype(F32).transpose(1, 0, 2, 3, 4)
    grads = grads.reshape(chunk * blks * tps * tok, part)
    total_ref[...] += jnp.dot(grads.T.astype(BF16), columns_ref[...], preferred_element_type=F32)

    @pl.when(step == pl.num_programs(0) - 1)
    def _():
        out_ref[...] = total_ref[...].T.astype(BF16)


def product(all_columns, arrived, steps):
    blks, slices, tps, tok, part = arrived.shape
    tokens, shard = all_columns.shape
    return pl.pallas_call(
        product_kernel,
        grid=(steps,),
        in_specs=[
            pl.BlockSpec((tokens // steps, shard), lambda i: (i, 0)),
            pl.BlockSpec((blks, slices // steps, tps, tok, part), lambda i: (0, i, 0, 0, 0)),
        ],
        out_specs=pl.BlockSpec((shard, part), lambda i: (0, 0)),
        out_shape=jax.ShapeDtypeStruct((shard, part), BF16),
        scratch_shapes=[pltpu.VMEM((part, shard), F32)],
        compiler_params=pltpu.CompilerParams(vmem_limit_bytes=55040 << 10),
        name="product",
    )(all_columns, arrived)


def gather_rows_kernel(own_rows, pieces_ref, out_ref):
    total = pieces_ref[0].astype(F32)
    for k in range(1, pieces_ref.shape[0]):
        total += pieces_ref[k].astype(F32)
    slices, padded, part = out_ref.shape
    squares = jnp.full((padded - own_rows, part), jnp.sum(total * total), F32)
    for j in range(slices):
        out_ref[j, :own_rows] = total[j * own_rows : (j + 1) * own_rows]
        out_ref[j, own_rows:] = squares


def gather_rows(pieces, own_rows, slices, padded):
    return pl.pallas_call(
        functools.partial(gather_rows_kernel, own_rows),
        out_shape=jax.ShapeDtypeStruct((slices, padded, pieces.shape[2]), F32),
        compiler_params=pltpu.CompilerParams(vmem_limit_bytes=12 << 20),
        name="gather_rows",
    )(pieces)


def squares_kernel(own_rows, back_ref, out_ref):
    total = jnp.sum(back_ref[:, own_rows : own_rows + 1, :], axis=0)
    out_ref[...] = jnp.broadcast_to(total[None], out_ref.shape)


def spread_squares(back, own_rows, size):
    return pl.pallas_call(
        functools.partial(squares_kernel, own_rows),
        out_shape=jax.ShapeDtypeStruct((size, 1, back.shape[2]), F32),
        compiler_params=pltpu.CompilerParams(vmem_limit_bytes=12 << 20),
        name="spread_squares",
    )(back)


def clip_kernel(limit_square, back_ref, squares_ref, out_ref, norm_ref):
    squares = jnp.sum(squares_ref[...], axis=0)
    norm = jnp.sqrt(squares)
    factor = jnp.minimum(1.0, jnp.sqrt(jnp.full_like(norm, limit_square)) / (norm + 1e-06))
    norm_ref[0, 0] = jnp.max(norm)
    slices, _, part = back_ref.shape
    for j in range(slices):
        for r in range(out_ref.shape[0]):
            out_ref[r, :, j * part : (j + 1) * part] = back_ref[j, r : r + 1, :] * factor


def clip(back, squares, own_rows, width, limit_square):
    return pl.pallas_call(
        functools.partial(clip_kernel, limit_square),
        out_shape=(
            jax.ShapeDtypeStruct((own_rows, 1, width), F32),
            jax.ShapeDtypeStruct((1, 1), F32),
        ),
        out_specs=(
            pl.BlockSpec(memory_space=pltpu.VMEM),
            pl.BlockSpec(memory_space=pltpu.SMEM),
        ),
        compiler_params=pltpu.CompilerParams(vmem_limit_bytes=12 << 20),
        name="clip",
    )(back, squares)


def body(hidden, projection_weight, norm_gain, upstream, loss_mask):
    tok, joined = hidden.shape
    groups = lax.axis_size(GROUP)
    shard, width = projection_weight.shape
    slices = YS * CORES
    part = width // slices
    own_rows = shard // (ZHI * slices)

    sent = lax.optimization_barrier(hidden.reshape(tok, groups, shard).transpose(1, 0, 2))
    offset = lax.axis_index(GROUP) * tok
    own_cotangent = lax.dynamic_slice_in_dim(upstream, offset, tok, 0)
    own_mask = lax.dynamic_slice_in_dim(loss_mask, offset, tok, 0)
    scaled = norm_gain * (own_cotangent.astype(F32) * own_mask.astype(F32)[:, None])
    columns = exchange(sent, GROUP)
    columns, scaled = lax.optimization_barrier((columns, scaled))
    columns = columns.reshape(groups * tok, shard)
    partial_value = jnp.dot(columns, projection_weight, preferred_element_type=F32).astype(BF16)
    columns, partial_value = lax.optimization_barrier((columns, partial_value))
    all_columns = lax.all_gather(columns, ALONG, axis=0, tiled=True)
    parts = exchange(lax.optimization_barrier(partial_value.reshape(groups, tok, width)), GROUP)

    blks, tps = lax.axis_size("blk"), lax.axis_size("tp")
    cut = norm_backward(parts, scaled, slices, tps).reshape(slices * tps, tok, part)
    cut = exchange(cut, ALONG + ("tp",))
    spread = lax.optimization_barrier(jnp.broadcast_to(cut[None], (blks, slices * tps, tok, part)))
    arrived = exchange(spread, "blk").reshape(blks, slices, tps, tok, part)
    block = product(all_columns, arrived, 2)
    by_zh = exchange(block.reshape(ZHI, shard // ZHI, part), "zh")

    back = exchange(gather_rows(by_zh, own_rows, slices, 16), ALONG)
    squares = exchange(spread_squares(back, own_rows, ZHI * groups), ("zh",) + GROUP)
    rows, grad_norm = clip(back, squares, own_rows, width, float(joined * width))
    return (rows.transpose(1, 0, 2), grad_norm.reshape(()))


def solution(mesh):
    sizes = (ZHI, YS, CORES, mesh.shape["blk"], mesh.shape["tp"])
    fine = Mesh(mesh.devices.reshape(sizes), REP + GROUP)
    return jax.shard_map(
        body,
        mesh=fine,
        in_specs=(
            P(REP + GROUP, None),
            P(GROUP, None),
            P(),
            P(REP, None),
            P(REP),
        ),
        out_specs=(P(GROUP, REP, None), P()),
        check_vma=False,
    )
```

```python
import functools

import jax
import jax.numpy as jnp
from jax import lax
from jax.experimental import pallas as pl
from jax.experimental.pallas import tpu as pltpu
from jax.sharding import Mesh, PartitionSpec as P

ZHI, YS, CORES = 4, 8, 2
REP = ("zh", "y", "core")
ALONG = ("y", "core")
GROUP = ("blk", "tp")
BF16, F32 = jnp.bfloat16, jnp.float32


def exchange(blocks, axes):
    return lax.all_to_all(blocks, axes, split_axis=0, concat_axis=0, tiled=True)


def norm_backward_kernel(parts_ref, scaled_ref, out_ref):
    groups = parts_ref.shape[0]
    projected = parts_ref[0].astype(F32)
    for g in range(1, groups):
        projected += parts_ref[g].astype(F32)
    scaled = scaled_ref[...]
    inverse_rms = lax.rsqrt(jnp.mean(projected * projected, axis=1, keepdims=True) + 1e-06)
    normed = projected * inverse_rms
    along = jnp.mean(scaled * normed, axis=1, keepdims=True)
    token_grad = (inverse_rms * (scaled - normed * along)).astype(BF16)
    cols = out_ref.shape[3]
    for j in range(out_ref.shape[0]):
        for k in range(out_ref.shape[1]):
            out_ref[j, k] = token_grad[:, j * cols : (j + 1) * cols]


def norm_backward(parts, scaled, slices, copies):
    _, tok, width = parts.shape
    return pl.pallas_call(
        norm_backward_kernel,
        out_shape=jax.ShapeDtypeStruct((slices, copies, tok, width // slices), BF16),
        compiler_params=pltpu.CompilerParams(vmem_limit_bytes=12 << 20),
        name="norm_backward",
    )(parts, scaled)


def product_kernel(columns_ref, grads_ref, keep_ref, give_ref, total_ref):
    step = pl.program_id(0)
    blks, chunk, tps, tok, cols = grads_ref.shape
    part = keep_ref.shape[1]
    grads = grads_ref[...].astype(F32).transpose(1, 0, 2, 3, 4)
    grads = grads.reshape(chunk * blks * tps * tok, cols).T.astype(BF16)
    term = jnp.dot(grads, columns_ref[...], preferred_element_type=F32)

    @pl.when(step == 0)
    def _():
        total_ref[...] = term

    @pl.when(step != 0)
    def _():
        total_ref[...] += term

    @pl.when(step == pl.num_programs(0) - 1)
    def _():
        core = lax.axis_index("core")
        keep_ref[...] = total_ref[pl.ds(pl.multiple_of(core * part, part), part)].T
        given = total_ref[pl.ds(pl.multiple_of((1 - core) * part, part), part)]
        give_ref[...] = given.T.astype(BF16)


def product(all_columns, arrived, steps):
    blks, ys, tps, tok, cols = arrived.shape
    tokens, shard = all_columns.shape
    half = (shard, cols // CORES)
    return pl.pallas_call(
        product_kernel,
        grid=(steps,),
        in_specs=[
            pl.BlockSpec((tokens // steps, shard), lambda i: (i, 0)),
            pl.BlockSpec((blks, ys // steps, tps, tok, cols), lambda i: (0, i, 0, 0, 0)),
        ],
        out_specs=[pl.BlockSpec(half, lambda i: (0, 0))] * 2,
        out_shape=[jax.ShapeDtypeStruct(half, F32), jax.ShapeDtypeStruct(half, BF16)],
        scratch_shapes=[pltpu.VMEM((cols, shard), F32)],
        compiler_params=pltpu.CompilerParams(vmem_limit_bytes=54528 << 10),
        name="product",
    )(all_columns, arrived)


def gather_rows_kernel(own_rows, pieces_ref, out_ref):
    total = pieces_ref[0].astype(F32)
    for k in range(1, pieces_ref.shape[0]):
        total += pieces_ref[k].astype(F32)
    slices, padded, part = out_ref.shape
    squares = jnp.full((padded - own_rows, part), jnp.sum(total * total), F32)
    for j in range(slices):
        out_ref[j, :own_rows] = total[j * own_rows : (j + 1) * own_rows]
        out_ref[j, own_rows:] = squares


def gather_rows(pieces, own_rows, slices, padded):
    return pl.pallas_call(
        functools.partial(gather_rows_kernel, own_rows),
        out_shape=jax.ShapeDtypeStruct((slices, padded, pieces.shape[2]), F32),
        compiler_params=pltpu.CompilerParams(vmem_limit_bytes=12 << 20),
        name="gather_rows",
    )(pieces)


def squares_kernel(own_rows, back_ref, out_ref):
    total = jnp.sum(back_ref[:, own_rows : own_rows + 1, :], axis=0)
    out_ref[...] = jnp.broadcast_to(total[None], out_ref.shape)


def spread_squares(back, own_rows, size):
    return pl.pallas_call(
        functools.partial(squares_kernel, own_rows),
        out_shape=jax.ShapeDtypeStruct((size, 1, back.shape[2]), F32),
        compiler_params=pltpu.CompilerParams(vmem_limit_bytes=12 << 20),
        name="spread_squares",
    )(back)


def clip_kernel(limit_square, back_ref, squares_ref, out_ref, norm_ref):
    squares = jnp.sum(squares_ref[...], axis=0)
    norm = jnp.sqrt(squares)
    factor = jnp.minimum(1.0, jnp.sqrt(jnp.full_like(norm, limit_square)) / (norm + 1e-06))
    norm_ref[0, 0] = jnp.max(norm)
    slices, _, part = back_ref.shape
    for j in range(slices):
        for r in range(out_ref.shape[0]):
            out_ref[r, :, j * part : (j + 1) * part] = back_ref[j, r : r + 1, :] * factor


def clip(back, squares, own_rows, width, limit_square):
    return pl.pallas_call(
        functools.partial(clip_kernel, limit_square),
        out_shape=(
            jax.ShapeDtypeStruct((own_rows, 1, width), F32),
            jax.ShapeDtypeStruct((1, 1), F32),
        ),
        out_specs=(
            pl.BlockSpec(memory_space=pltpu.VMEM),
            pl.BlockSpec(memory_space=pltpu.SMEM),
        ),
        compiler_params=pltpu.CompilerParams(vmem_limit_bytes=12 << 20),
        name="clip",
    )(back, squares)


def body(hidden, projection_weight, norm_gain, upstream, loss_mask):
    tok, joined = hidden.shape
    groups = lax.axis_size(GROUP)
    shard, width = projection_weight.shape
    slices = YS * CORES
    part = width // slices
    own_rows = shard // (ZHI * slices)

    sent = lax.optimization_barrier(hidden.reshape(tok, groups, shard).transpose(1, 0, 2))
    offset = lax.axis_index(GROUP) * tok
    own_cotangent = lax.dynamic_slice_in_dim(upstream, offset, tok, 0)
    own_mask = lax.dynamic_slice_in_dim(loss_mask, offset, tok, 0)
    scaled = norm_gain * (own_cotangent.astype(F32) * own_mask.astype(F32)[:, None])
    columns = exchange(sent, GROUP)
    columns, scaled = lax.optimization_barrier((columns, scaled))
    columns = columns.reshape(groups * tok, shard)
    partial_value = jnp.dot(columns, projection_weight, preferred_element_type=F32).astype(BF16)
    columns, partial_value = lax.optimization_barrier((columns, partial_value))
    all_columns = lax.all_gather(columns, "y", axis=0, tiled=True)
    parts = exchange(lax.optimization_barrier(partial_value.reshape(groups, tok, width)), GROUP)

    blks, tps, cols = lax.axis_size("blk"), lax.axis_size("tp"), CORES * part
    cut = norm_backward(parts, scaled, YS, tps).reshape(YS * tps, tok, cols)
    cut = exchange(cut, ("y", "tp"))
    spread = lax.optimization_barrier(jnp.broadcast_to(cut[None], (blks, YS * tps, tok, cols)))
    arrived = exchange(spread, "blk").reshape(blks, YS, tps, tok, cols)
    keep, give = product(all_columns, arrived, 2)
    block = (keep + lax.ppermute(give, "core", [(0, 1), (1, 0)]).astype(F32)).astype(BF16)
    by_zh = exchange(block.reshape(ZHI, shard // ZHI, part), "zh")

    back = exchange(gather_rows(by_zh, own_rows, slices, 16), ALONG)
    squares = exchange(spread_squares(back, own_rows, ZHI * groups), ("zh",) + GROUP)
    rows, grad_norm = clip(back, squares, own_rows, width, float(joined * width))
    return (rows.transpose(1, 0, 2), grad_norm.reshape(()))


def solution(mesh):
    sizes = (ZHI, YS, CORES, mesh.shape["blk"], mesh.shape["tp"])
    fine = Mesh(mesh.devices.reshape(sizes), REP + GROUP)
    return jax.shard_map(
        body,
        mesh=fine,
        in_specs=(
            P(REP + GROUP, None),
            P(GROUP, None),
            P(),
            P(REP, None),
            P(REP),
        ),
        out_specs=(P(GROUP, REP, None), P()),
        check_vma=False,
    )
```

```python
import functools

import jax
import jax.numpy as jnp
from jax import lax
from jax.experimental import pallas as pl
from jax.experimental.pallas import tpu as pltpu
from jax.sharding import Mesh, PartitionSpec as P

ZHI, YS, CORES = 4, 8, 2
REP = ("zh", "y", "core")
ALONG = ("y", "core")
GROUP = ("blk", "tp")
LANES = 128
BF16, F32 = jnp.bfloat16, jnp.float32


def exchange(blocks, axes):
    return lax.all_to_all(blocks, axes, split_axis=0, concat_axis=0, tiled=True)


def norm_backward_kernel(parts_ref, scaled_ref, out_ref):
    groups = parts_ref.shape[0]
    projected = parts_ref[0].astype(F32)
    for g in range(1, groups):
        projected += parts_ref[g].astype(F32)
    scaled = scaled_ref[...]
    inverse_rms = lax.rsqrt(jnp.mean(projected * projected, axis=1, keepdims=True) + 1e-06)
    normed = projected * inverse_rms
    along = jnp.mean(scaled * normed, axis=1, keepdims=True)
    token_grad = (inverse_rms * (scaled - normed * along)).astype(BF16)
    for j in range(out_ref.shape[0]):
        for k in range(out_ref.shape[1]):
            out_ref[j, k] = token_grad[:, j * LANES : (j + 1) * LANES]


def norm_backward(parts, scaled, slices, copies):
    _, tok, width = parts.shape
    return pl.pallas_call(
        norm_backward_kernel,
        out_shape=jax.ShapeDtypeStruct((slices, copies, tok, width // slices), BF16),
        compiler_params=pltpu.CompilerParams(vmem_limit_bytes=12 << 20),
        name="norm_backward",
    )(parts, scaled)


def product_kernel(columns_ref, grads_ref, out_ref, total_ref):
    step = pl.program_id(0)

    @pl.when(step == 0)
    def _():
        total_ref[...] = jnp.zeros_like(total_ref)

    blks, chunk, tps, tok, part = grads_ref.shape
    grads = grads_ref[...].astype(F32).transpose(1, 0, 2, 3, 4)
    grads = grads.reshape(chunk * blks * tps * tok, part)
    total_ref[...] += jnp.dot(grads.T.astype(BF16), columns_ref[...], preferred_element_type=F32)

    @pl.when(step == pl.num_programs(0) - 1)
    def _():
        out_ref[...] = total_ref[...].T.astype(BF16)


def product(all_columns, arrived, steps):
    blks, slices, tps, tok, part = arrived.shape
    tokens, shard = all_columns.shape
    return pl.pallas_call(
        product_kernel,
        grid=(steps,),
        in_specs=[
            pl.BlockSpec((tokens // steps, shard), lambda i: (i, 0)),
            pl.BlockSpec((blks, slices // steps, tps, tok, part), lambda i: (0, i, 0, 0, 0)),
        ],
        out_specs=pl.BlockSpec((shard, part), lambda i: (0, 0)),
        out_shape=jax.ShapeDtypeStruct((shard, part), BF16),
        scratch_shapes=[pltpu.VMEM((part, shard), F32)],
        compiler_params=pltpu.CompilerParams(vmem_limit_bytes=55040 << 10),
        name="product",
    )(all_columns, arrived)


def gather_rows_kernel(own_rows, pieces_ref, out_ref):
    total = pieces_ref[0].astype(F32)
    for k in range(1, pieces_ref.shape[0]):
        total += pieces_ref[k].astype(F32)
    slices, padded, part = out_ref.shape
    squares = jnp.full((padded - own_rows, part), jnp.sum(total * total), F32)
    for j in range(slices):
        out_ref[j, :own_rows] = total[j * own_rows : (j + 1) * own_rows]
        out_ref[j, own_rows:] = squares


def gather_rows(pieces, own_rows, slices, padded):
    return pl.pallas_call(
        functools.partial(gather_rows_kernel, own_rows),
        out_shape=jax.ShapeDtypeStruct((slices, padded, pieces.shape[2]), F32),
        compiler_params=pltpu.CompilerParams(vmem_limit_bytes=12 << 20),
        name="gather_rows",
    )(pieces)


def squares_kernel(own_rows, back_ref, out_ref):
    total = jnp.sum(back_ref[:, own_rows : own_rows + 1, :], axis=0)
    out_ref[...] = jnp.broadcast_to(total[None], out_ref.shape)


def spread_squares(back, own_rows, size):
    return pl.pallas_call(
        functools.partial(squares_kernel, own_rows),
        out_shape=jax.ShapeDtypeStruct((size, 1, back.shape[2]), F32),
        compiler_params=pltpu.CompilerParams(vmem_limit_bytes=12 << 20),
        name="spread_squares",
    )(back)


def clip_kernel(limit_square, back_ref, squares_ref, out_ref, norm_ref):
    squares = jnp.sum(squares_ref[...], axis=0)
    norm = jnp.sqrt(squares)
    factor = jnp.minimum(1.0, jnp.sqrt(jnp.full_like(norm, limit_square)) / (norm + 1e-06))
    norm_ref[0, 0] = jnp.max(norm)
    slices, _, part = back_ref.shape
    for j in range(slices):
        for r in range(out_ref.shape[0]):
            out_ref[r, :, j * part : (j + 1) * part] = back_ref[j, r : r + 1, :] * factor


def clip(back, squares, own_rows, width, limit_square):
    return pl.pallas_call(
        functools.partial(clip_kernel, limit_square),
        out_shape=(
            jax.ShapeDtypeStruct((own_rows, 1, width), F32),
            jax.ShapeDtypeStruct((1, 1), F32),
        ),
        out_specs=(
            pl.BlockSpec(memory_space=pltpu.VMEM),
            pl.BlockSpec(memory_space=pltpu.SMEM),
        ),
        compiler_params=pltpu.CompilerParams(vmem_limit_bytes=12 << 20),
        name="clip",
    )(back, squares)


def body(hidden, projection_weight, norm_gain, upstream, loss_mask):
    tok, joined = hidden.shape
    groups = lax.axis_size(GROUP)
    shard, width = projection_weight.shape
    slices = YS * CORES
    part = width // slices
    own_rows = shard // (ZHI * slices)

    sent = lax.optimization_barrier(hidden.reshape(tok, groups, shard).transpose(1, 0, 2))
    offset = lax.axis_index(GROUP) * tok
    own_cotangent = lax.dynamic_slice_in_dim(upstream, offset, tok, 0)
    own_mask = lax.dynamic_slice_in_dim(loss_mask, offset, tok, 0)
    scaled = norm_gain * (own_cotangent.astype(F32) * own_mask.astype(F32)[:, None])
    columns = exchange(sent, GROUP)
    columns, scaled = lax.optimization_barrier((columns, scaled))
    columns = columns.reshape(groups * tok, shard)
    all_columns = lax.all_gather(columns, ALONG, axis=0, tiled=True)
    partial_value = jnp.dot(columns, projection_weight, preferred_element_type=F32).astype(BF16)
    parts = exchange(lax.optimization_barrier(partial_value.reshape(groups, tok, width)), GROUP)

    blks, tps = lax.axis_size("blk"), lax.axis_size("tp")
    cut = norm_backward(parts, scaled, slices, tps).reshape(slices * tps, tok, part)
    cut = exchange(cut, ALONG + ("tp",))
    spread = lax.optimization_barrier(jnp.broadcast_to(cut[None], (blks, slices * tps, tok, part)))
    arrived = exchange(spread, "blk").reshape(blks, slices, tps, tok, part)
    block = product(all_columns, arrived, 2)
    by_zh = exchange(block.reshape(ZHI, shard // ZHI, part), "zh")

    back = exchange(gather_rows(by_zh, own_rows, slices, 16), ALONG)
    squares = exchange(spread_squares(back, own_rows, ZHI * groups), ("zh",) + GROUP)
    rows, grad_norm = clip(back, squares, own_rows, width, float(joined * width))
    return (rows.transpose(1, 0, 2), grad_norm.reshape(()))


def solution(mesh):
    sizes = (ZHI, YS, CORES, mesh.shape["blk"], mesh.shape["tp"])
    fine = Mesh(mesh.devices.reshape(sizes), REP + GROUP)
    return jax.shard_map(
        body,
        mesh=fine,
        in_specs=(
            P(REP + GROUP, None),
            P(GROUP, None),
            P(),
            P(REP, None),
            P(REP),
        ),
        out_specs=(P(GROUP, REP, None), P()),
        check_vma=False,
    )
```
